256 devices in a mesh: head: 16 (over x_lo, y, core), ctx: 16 (over x_hi, z).
Axes of the slice: x: 4 (x_hi: 2, x_lo: 2; x = x_hi * 2 + x_lo), y: 4, z: 8, core: 2. Of those that a mesh axis runs over, the one named last changes fastest.
Arguments:
- query_states: bfloat16 [16384, 8192], P(('head', 'ctx')), may hold values from -6 to 6
- saved_key_rows: bfloat16 [16384, 1024], P(('head', 'ctx')), may hold values from -6 to 6
- saved_value_rows: bfloat16 [16384, 1024], P(('head', 'ctx')), may hold values from -6 to 6
- attn_output: bfloat16 [16384, 8192], P(('head', 'ctx')), may hold values from -3 to 3
- out_grad: bfloat16 [16384, 8192], P(('head', 'ctx')), may hold values from -6 to 6
- log_norm: float32 [16384, 64], P(('head', 'ctx')), may hold values from 4 to 6
- block_pos: int32 [256], replicated, may hold values from 0 to 255, as said below
Outputs:
- query_grad: bfloat16 [16384, 8192], P(('head', 'ctx'))
- key_gradient: bfloat16 [16384, 1024], P(('head', 'ctx'))
- value_gradient: bfloat16 [16384, 1024], P(('head', 'ctx'))
The draws below stay inside these ranges and needn't reach their ends.
Inputs may be any that keep to these rules, and one draw needn't show every extreme that they name: block_pos is a permutation. For each c below 16 there is an r, different for different c, such that block c + j * 16 has position r * 8 + j for j below 8, and position (31 - r) * 8 + j - 8 for the other j.
All inputs are finite; a program needn't handle non-finite values.
Results may differ from the reference program's by a relative error of at most 0.0059.
Values may be sent and summed in bfloat16 or wider, within the bound.
A program may use at most 128 MiB of HBM per device.

```python
import jax
import jax.numpy as jnp
from jax import lax

HQ = 64
KEY_VALUE_HEADS = 8
HEAD_SIZE = 128
BLOCK = 64
CYCLE = 2
SEQUENCE_TOKENS = 16384
N_HEAD = 16
N_CTX = 16


def draw_block_pos(key, part):
    key = jax.random.fold_in(key, 7)
    ordering = jax.random.permutation(key, jnp.arange(N_CTX, dtype=jnp.int32))
    run_len = N_HEAD // 2
    member = jnp.arange(N_HEAD, dtype=jnp.int32)[:, None]
    run_index = ordering[None, :]
    early_run = run_index * run_len + member
    late_run = (2 * N_CTX - 1 - run_index) * run_len + member - run_len
    return jnp.where(member < run_len, early_run, late_run).reshape(N_HEAD * N_CTX).astype(jnp.int32)


def block_levels(rng, dims, split, low, high):
    def one(dim, blocks):
        steps = jax.random.uniform(jax.random.fold_in(jax.random.fold_in(rng, 6), dim), (blocks,), jnp.float32, low / len(split), high / len(split))
        return jnp.repeat(jnp.exp(steps), dims[dim] // blocks).reshape((-1,) + (1,) * (len(dims) - dim - 1))

    level = one(*split[0])
    for cut in split[1:]:
        level = level * one(*cut)
    return level


def normal_values(rng, extent, deviation, bound, pieces=(), held_as=jnp.bfloat16):
    level = block_levels(rng, extent, pieces, -0.22, 0.18) if pieces else 1.0
    result = jax.random.normal(rng, extent, jnp.float32) * deviation * level
    return jnp.minimum(jnp.maximum(result, -bound), bound).astype(held_as)


def setup_inputs(seed: int = 0) -> dict:
    key_of = jax.random.split(jax.random.key(seed), 8)
    query_states = normal_values(key_of[0], (SEQUENCE_TOKENS, HQ * HEAD_SIZE), 1.0, 6.0, ((0, 256),))
    saved_key_rows = normal_values(key_of[1], (SEQUENCE_TOKENS, KEY_VALUE_HEADS * HEAD_SIZE), 1.0, 6.0, ((0, 256),))
    saved_value_rows = normal_values(key_of[2], (SEQUENCE_TOKENS, KEY_VALUE_HEADS * HEAD_SIZE), 1.0, 6.0, ((0, 256),))
    attn_output = normal_values(key_of[3], (SEQUENCE_TOKENS, HQ * HEAD_SIZE), 0.5, 3.0, ((0, 256),))
    out_grad = normal_values(key_of[4], (SEQUENCE_TOKENS, HQ * HEAD_SIZE), 1.0, 6.0, ((0, 256),))
    log_norm = jnp.clip(4.0 + 2.0 * jax.random.uniform(key_of[5], (SEQUENCE_TOKENS, HQ), jnp.float32) ** block_levels(key_of[5], (SEQUENCE_TOKENS, HQ), ((0, 256),), -0.2, 0.2), 4.0, 6.0)
    block_pos = draw_block_pos(jax.random.fold_in(key_of[7], 71), 0)
    return {"query_states": query_states, "saved_key_rows": saved_key_rows, "saved_value_rows": saved_value_rows, "attn_output": attn_output, "out_grad": out_grad, "log_norm": log_norm, "block_pos": block_pos}


def tile_terms(q_blk, do_blk, norm_blk, delta_blk, k_blk, v_blk, q_pos, k_pos, factor):
    q_wide = q_blk.astype(jnp.float32)
    do_wide = do_blk.astype(jnp.float32)
    k_wide = k_blk.astype(jnp.float32)
    v_wide = v_blk.astype(jnp.float32)
    scores = jnp.einsum("qhd,kd->hqk", q_wide, k_wide) * factor
    visible = (q_pos[:, None] >= k_pos[None, :])[None]
    probs_f = jnp.where(visible, jnp.exp(scores - jnp.transpose(norm_blk)[:, :, None]), 0.0)
    grad_probs = jnp.einsum("qhd,kd->hqk", do_wide, v_wide)
    grad_score = (probs_f * (grad_probs - jnp.transpose(delta_blk)[:, :, None])).astype(jnp.bfloat16)
    probs_b = probs_f.astype(jnp.bfloat16)
    grad_score = lax.optimization_barrier(grad_score).astype(jnp.float32)
    probs_b = lax.optimization_barrier(probs_b).astype(jnp.float32)
    q_term = jnp.einsum("hqk,kd->qhd", grad_score, k_wide) * factor
    k_term = jnp.einsum("hqk,qhd->kd", grad_score, q_wide) * factor
    v_term = jnp.einsum("hqk,qhd->kd", probs_b, do_wide)
    return q_term, k_term, v_term


def gather_groups(array, width):
    return array.reshape(N_HEAD, N_CTX, BLOCK, width).transpose(1, 0, 2, 3).reshape(N_CTX, N_HEAD * BLOCK, width)


def spread_groups(array):
    width = array.shape[-1]
    return array.reshape(N_CTX, N_HEAD, BLOCK, width).transpose(1, 0, 2, 3).reshape(SEQUENCE_TOKENS, width)


def reference(query_states, saved_key_rows, saved_value_rows, attn_output, out_grad, log_norm, block_pos):
    sequence_row_count = N_HEAD * BLOCK
    heads_dev = HQ // N_HEAD
    repeat_factor = N_HEAD // KEY_VALUE_HEADS
    factor = HEAD_SIZE ** -0.5
    row_delta = jnp.sum((out_grad.astype(jnp.float32) * attn_output.astype(jnp.float32)).reshape(SEQUENCE_TOKENS, HQ, HEAD_SIZE), axis=2)
    q_group = gather_groups(query_states, HQ * HEAD_SIZE).reshape(N_CTX, sequence_row_count, N_HEAD, heads_dev, HEAD_SIZE).transpose(2, 0, 1, 3, 4)
    do_group = gather_groups(out_grad, HQ * HEAD_SIZE).reshape(N_CTX, sequence_row_count, N_HEAD, heads_dev, HEAD_SIZE).transpose(2, 0, 1, 3, 4)
    norm_group = gather_groups(log_norm, HQ).reshape(N_CTX, sequence_row_count, N_HEAD, heads_dev).transpose(2, 0, 1, 3)
    delta_group = gather_groups(row_delta, HQ).reshape(N_CTX, sequence_row_count, N_HEAD, heads_dev).transpose(2, 0, 1, 3)
    key_group_rows = gather_groups(saved_key_rows, KEY_VALUE_HEADS * HEAD_SIZE).reshape(N_CTX, sequence_row_count, KEY_VALUE_HEADS, HEAD_SIZE).transpose(2, 0, 1, 3)
    value_group_rows = gather_groups(saved_value_rows, KEY_VALUE_HEADS * HEAD_SIZE).reshape(N_CTX, sequence_row_count, KEY_VALUE_HEADS, HEAD_SIZE).transpose(2, 0, 1, 3)
    offsets = jnp.arange(BLOCK, dtype=jnp.int32)
    positions = (jnp.transpose(block_pos.reshape(N_HEAD, N_CTX))[:, :, None] * BLOCK + offsets[None, None, :]).reshape(N_CTX, sequence_row_count)

    def subgroup(member):
        k_head = key_group_rows[member // repeat_factor]
        v_head = value_group_rows[member // repeat_factor]
        q_member = q_group[member]
        do_member = do_group[member]
        norm_member = norm_group[member]
        delta_member = delta_group[member]

        def per_ctx(carry, ctx_index):
            k_acc, v_acc = carry
            q_acc = jnp.zeros((sequence_row_count, heads_dev, HEAD_SIZE), jnp.float32)
            for step in range(CYCLE):
                source = (ctx_index - step) % N_CTX
                q_term, k_term, v_term = tile_terms(q_member[ctx_index], do_member[ctx_index], norm_member[ctx_index], delta_member[ctx_index], k_head[source], v_head[source], positions[ctx_index], positions[source], factor)
                q_acc = q_acc + q_term
                k_acc = k_acc.at[source].add(k_term)
                v_acc = v_acc.at[source].add(v_term)
            return (k_acc, v_acc), q_acc.astype(jnp.bfloat16)

        zeros = jnp.zeros((N_CTX, sequence_row_count, HEAD_SIZE), jnp.float32)
        (k_acc, v_acc), q_out = lax.scan(per_ctx, (zeros, zeros), jnp.arange(N_CTX, dtype=jnp.int32))
        return q_out, k_acc.astype(jnp.bfloat16), v_acc.astype(jnp.bfloat16)

    q_parts, k_parts, v_parts = lax.map(subgroup, jnp.arange(N_HEAD, dtype=jnp.int32))
    query_grad = spread_groups(q_parts.transpose(1, 2, 0, 3, 4).reshape(N_CTX, sequence_row_count, HQ * HEAD_SIZE))

    def combine(sequence_pieces):
        summed_result = jnp.sum(sequence_pieces.astype(jnp.float32).reshape(KEY_VALUE_HEADS, repeat_factor, N_CTX, sequence_row_count, HEAD_SIZE), axis=1).astype(jnp.bfloat16)
        return spread_groups(summed_result.transpose(1, 2, 0, 3).reshape(N_CTX, sequence_row_count, KEY_VALUE_HEADS * HEAD_SIZE))

    return query_grad, combine(k_parts), combine(v_parts)
```

```python
import jax
import jax.numpy as jnp
from jax import lax
from jax.experimental import pallas as pl
from jax.experimental.pallas import tpu as pltpu
from jax.sharding import PartitionSpec as P

HQ = 64
KEY_VALUE_HEADS = 8
HEAD_SIZE = 128
BLOCK = 64
N = 16
HEADS = HQ // N
ROWS = N * BLOCK
HALF = ROWS // 2
QUARTER = ROWS // 4
FACTOR = HEAD_SIZE**-0.5
LOG2E = 1.4426950408889634
MESH = pl.DeviceIdType.MESH
F32 = jnp.float32
BF16 = jnp.bfloat16


def dot(a, b):
    return jnp.dot(a, b, preferred_element_type=F32)


def dot_t(a, b):
    return lax.dot_general(a, b, (((1,), (1,)), ((), ())), preferred_element_type=F32)


def transposed(x):
    return x.astype(F32).T.astype(BF16)


def tile(k, kt, v, q, do, norm, delta, diagonal):
    s = dot_t(k, q)
    p = jnp.exp2(s * (FACTOR * LOG2E) - norm)
    if diagonal:
        key = lax.broadcasted_iota(jnp.int32, s.shape, 0)
        query = lax.broadcasted_iota(jnp.int32, s.shape, 1)
        p = jnp.where(query >= key, p, 0.0)
    ds = (p * (dot_t(v, do) - delta)).astype(BF16)
    return dot(kt, ds), dot(ds, q), dot(p.astype(BF16), do)


def kernel(
    q, do, at, k, v, ln, bp,
    qg, kvg,
    dov, atv, kvs, st_s, st_r, srow, qd, own, prev, own_t, prev_t, sel, sel_t,
    acc_own, acc_prev, acc_sel, dq_t, dq_s, x_s, x_r, ctx_s, ctx_r, y_s, y_r, fin,
    s_load, s_kv, r_kv, s_fw, r_fw, s_ctx, r_ctx, s_fwp, r_fwp, s_st, r_st, s_qd, r_qd,
    s_x, r_x, s_back, r_back, s_y, r_y, s_dq, r_dq, s_fin, r_fin,
):
    h = lax.axis_index("head")
    c = lax.axis_index("ctx")
    g = lax.div(h, 2)
    m = lax.rem(h, 2)
    mate = h + 1 - 2 * m
    after = lax.rem(c + 1, N)
    before = lax.rem(c + N - 1, N)

    def remote(src, dst, ssem, rsem, **where):
        return pltpu.make_async_remote_copy(
            src_ref=src, dst_ref=dst, send_sem=ssem, recv_sem=rsem, device_id=where, device_id_type=MESH
        )

    def wait(ref, sem):
        pltpu.make_async_copy(ref, ref, sem).wait()

    def cols(j):
        return pl.ds(pl.multiple_of(j * HEAD_SIZE, HEAD_SIZE), HEAD_SIZE)

    def rows(j):
        return pl.ds(pl.multiple_of(j * BLOCK, BLOCK), BLOCK)

    loads = [
        pltpu.make_async_copy(k, kvs.at[0], s_load.at[0]),
        pltpu.make_async_copy(v, kvs.at[1], s_load.at[1]),
        pltpu.make_async_copy(do, dov, s_load.at[2]),
        pltpu.make_async_copy(at, atv, s_load.at[3]),
    ]
    for copy in loads:
        copy.start()

    barrier = pltpu.get_barrier_semaphore()

    @pl.loop(1, N)
    def _(s):
        pl.semaphore_signal(barrier, inc=1, device_id={"head": lax.rem(h + s, N)}, device_id_type=MESH)

    pl.semaphore_signal(barrier, inc=1, device_id={"ctx": after}, device_id_type=MESH)
    pl.semaphore_signal(barrier, inc=1, device_id={"ctx": before}, device_id_type=MESH)
    loads[0].wait()
    loads[1].wait()
    pl.semaphore_wait(barrier, N + 1)

    @pl.loop(1, N)
    def _(s):
        d = lax.rem(h + s, N)
        e = lax.rem(d, 2)
        remote(kvs.at[e, :, cols(lax.div(d, 2))], own.at[e, rows(h)], s_kv, r_kv, head=d).start()

    pltpu.make_async_copy(kvs.at[m, :, cols(g)], own.at[m, rows(h)], r_kv).start()

    def send_head(i):
        @pl.loop(1, N)
        def _(s):
            d = lax.rem(h + s, N)
            for which, ref in ((0, q), (1, do)):
                remote(
                    ref.at[:, cols(d * HEADS + i)], qd.at[i, which, rows(h)], s_qd.at[i], r_qd.at[i], head=d
                ).start()

        for which, ref in ((0, q), (1, do)):
            pltpu.make_async_copy(ref.at[:, cols(h * HEADS + i)], qd.at[i, which, rows(h)], r_qd.at[i]).start()

    send_head(0)

    loads[2].wait()
    loads[3].wait()
    lane = lax.broadcasted_iota(jnp.int32, (BLOCK, 2 * BLOCK), 1)

    def inner(j, total):
        part = jnp.sum(dov[:, cols(j)].astype(F32) * atv[:, cols(j)].astype(F32), axis=1, keepdims=True)
        return jnp.where(lane == j, part, total)

    deltas = lax.fori_loop(0, HQ, inner, jnp.zeros((BLOCK, 2 * BLOCK), F32), unroll=8)
    stats = jnp.where(lane < BLOCK, deltas, jnp.concatenate([ln[...], ln[...]], axis=1) * LOG2E).T
    stats = jnp.concatenate([stats, stats], axis=1)
    for d in range(N):
        st_s[d, 0:HEADS] = stats[HQ + d * HEADS : HQ + (d + 1) * HEADS]
        st_s[d, HEADS:] = stats[d * HEADS : (d + 1) * HEADS]

    @pl.loop(1, N)
    def _(s):
        d = lax.rem(h + s, N)
        remote(st_s.at[d], st_r.at[h], s_st, r_st, head=d).start()

    pltpu.make_async_copy(st_s.at[h], st_r.at[h], r_st).start()

    @pl.loop(1, HEADS)
    def _(i):
        send_head(i)

    wait(own.at[0], r_kv)
    forward = remote(own.at[m], own.at[m], s_fw, r_fw, head=mate)
    forward.start()
    onward = remote(own.at[m], prev.at[m], s_ctx, r_ctx, ctx=after)
    onward.start()
    forward.wait_recv()
    own_t[...] = transposed(own[0])

    wait(st_r, r_st)
    wide = lax.broadcasted_iota(jnp.int32, (2 * HEADS, 2 * BLOCK), 1)
    for pair in range(N // 2):
        srow[:, pair * 128 : (pair + 1) * 128] = jnp.where(wide < BLOCK, st_r[2 * pair], st_r[2 * pair + 1])

    onward.wait_recv()
    forward_prev = remote(prev.at[m], prev.at[m], s_fwp, r_fwp, head=mate)
    forward_prev.start()
    acc_own[...] = jnp.zeros_like(acc_own)
    acc_prev[...] = jnp.zeros_like(acc_prev)
    acc_sel[...] = jnp.zeros_like(acc_sel)
    forward_prev.wait_recv()

    early = bp[c] > bp[before]
    for which in range(2):
        sel[which] = jnp.where(early, prev[which, :HALF], prev[which, HALF:])
    prev_t[...] = transposed(prev[0, :HALF])
    sel_t[...] = transposed(sel[0])

    def add(ref, lo, size, dk, dv):
        ref[0, lo : lo + size] += dk
        ref[1, lo : lo + size] += dv

    def row(i, lo, size):
        return srow[pl.ds(i, 1), lo : lo + size], srow[pl.ds(HEADS + i, 1), lo : lo + size]

    def combined(which):
        chosen = acc_sel[which]
        zero = jnp.zeros_like(chosen)
        low = acc_prev[which] + jnp.where(early, chosen, zero)
        return low, jnp.where(early, zero, chosen)

    @pl.loop(0, HEADS)
    def _(i):
        wait(qd.at[i], r_qd.at[i])
        q_sel = jnp.where(early, qd[i, 0, :HALF], qd[i, 0, HALF:])
        do_sel = jnp.where(early, qd[i, 1, :HALF], qd[i, 1, HALF:])
        n0, d0 = row(i, 0, HALF)
        n1, d1 = row(i, HALF, HALF)
        dq, dk, dv = tile(
            sel[0], sel_t[...], sel[1], q_sel, do_sel, jnp.where(early, n0, n1), jnp.where(early, d0, d1), False
        )
        add(acc_sel, 0, HALF, dk, dv)
        zero = jnp.zeros_like(dq)
        dq_t[:, :HALF] = jnp.where(early, dq, zero)
        dq_t[:, HALF:] = jnp.where(early, zero, dq)
        dq, dk, dv = tile(
            prev[0, :HALF], prev_t[...], prev[1, :HALF], qd[i, 0, HALF:], qd[i, 1, HALF:], n1, d1, False
        )
        add(acc_prev, 0, HALF, dk, dv)
        dq_t[:, HALF:] += dq

        @pl.when(i == HEADS - 1)
        def _():
            low, high = combined(1 - m)
            x_s[:HALF] = low.astype(BF16)
            x_s[HALF:] = high.astype(BF16)
            remote(x_s, x_r, s_x, r_x, head=mate).start()

        dq, dk, dv = tile(
            own[0, :HALF], own_t[:, :HALF], own[1, :HALF], qd[i, 0, HALF:], qd[i, 1, HALF:], n1, d1, False
        )
        add(acc_own, 0, HALF, dk, dv)
        dq_t[:, HALF:] += dq

        @pl.when(i == HEADS - 1)
        def _():
            wait(x_r, r_x)
            low, high = combined(m)
            scale = jnp.where(m == 0, FACTOR, 1.0)
            ctx_s[:HALF] = ((low + x_r[:HALF].astype(F32)) * scale).astype(BF16)
            ctx_s[HALF:] = ((high + x_r[HALF:].astype(F32)) * scale).astype(BF16)
            remote(ctx_s, ctx_r, s_back, r_back, ctx=before).start()

        for kb, qb, size in ((0, 0, 1), (0, 1, 1), (1, 1, 1), (2, 2, 1), (2, 3, 1), (3, 3, 1)):
            ks = slice(kb * QUARTER, (kb + size) * QUARTER)
            qs = slice(qb * QUARTER, (qb + size) * QUARTER)
            nn, dd = row(i, qb * QUARTER, QUARTER)
            dq, dk, dv = tile(own[0, ks], own_t[:, ks], own[1, ks], qd[i, 0, qs], qd[i, 1, qs], nn, dd, kb == qb)
            add(acc_own, kb * QUARTER, QUARTER, dk, dv)
            dq_t[:, qs] += dq

        dq_s[i] = (dq_t[...] * FACTOR).T.astype(BF16)

        @pl.loop(1, N)
        def _(s):
            d = lax.rem(h + s, N)
            remote(dq_s.at[i, rows(d)], qg.at[:, cols(h * HEADS + i)], s_dq, r_dq, head=d).start()

        pltpu.make_async_copy(dq_s.at[i, rows(h)], qg.at[:, cols(h * HEADS + i)], r_dq).start()

    y_s[...] = acc_own[1 - m].astype(BF16)
    remote(y_s, y_r, s_y, r_y, head=mate).start()
    wait(y_r, r_y)
    wait(ctx_r, r_back)
    scale = jnp.where(m == 0, FACTOR, 1.0)
    fin[...] = ((acc_own[m] + y_r[...].astype(F32)) * scale + ctx_r[...].astype(F32)).astype(BF16)

    @pl.loop(1, N)
    def _(s):
        d = lax.rem(h + s, N)
        remote(fin.at[rows(d)], kvg.at[m, :, cols(g)], s_fin, r_fin, head=d).start()

    pltpu.make_async_copy(fin.at[rows(h)], kvg.at[m, :, cols(g)], r_fin).start()

    most = (N - 1) * BLOCK
    wait(own.at[0, :most], s_kv)
    forward.wait_send()
    onward.wait_send()
    forward_prev.wait_send()
    wait(st_r.at[: N - 1], s_st)
    for i in range(HEADS):
        wait(qd.at[i, :, :most], s_qd.at[i])
    wait(x_s, s_x)
    wait(ctx_s, s_back)
    wait(y_s, s_y)
    wait(dq_s.at[:, :most], s_dq)
    wait(fin.at[:most], s_fin)
    wait(qg, r_dq)
    wait(kvg, r_fin)


def shards(query_states, saved_key_rows, saved_value_rows, attn_output, out_grad, log_norm, block_pos):
    hbm = pl.BlockSpec(memory_space=pl.ANY)
    dma = pltpu.SemaphoreType.DMA
    half = lambda *lead: pltpu.VMEM((*lead, HALF, HEAD_SIZE), BF16)
    full = lambda *lead: pltpu.VMEM((*lead, ROWS, HEAD_SIZE), BF16)
    qg, kvg = pl.pallas_call(
        kernel,
        out_shape=(
            jax.ShapeDtypeStruct((BLOCK, HQ * HEAD_SIZE), BF16),
            jax.ShapeDtypeStruct((2, BLOCK, KEY_VALUE_HEADS * HEAD_SIZE), BF16),
        ),
        in_specs=[hbm] * 5 + [pl.BlockSpec(memory_space=pltpu.VMEM), pl.BlockSpec(memory_space=pltpu.SMEM)],
        out_specs=(hbm, hbm),
        scratch_shapes=[
            pltpu.VMEM((BLOCK, HQ * HEAD_SIZE), BF16),
            pltpu.VMEM((BLOCK, HQ * HEAD_SIZE), BF16),
            pltpu.VMEM((2, BLOCK, KEY_VALUE_HEADS * HEAD_SIZE), BF16),
            pltpu.VMEM((N, 2 * HEADS, 2 * BLOCK), F32),
            pltpu.VMEM((N, 2 * HEADS, 2 * BLOCK), F32),
            pltpu.VMEM((2 * HEADS, ROWS), F32),
            full(HEADS, 2),
            full(2),
            full(2),
            pltpu.VMEM((HEAD_SIZE, ROWS), BF16),
            pltpu.VMEM((HEAD_SIZE, HALF), BF16),
            half(2),
            pltpu.VMEM((HEAD_SIZE, HALF), BF16),
            pltpu.VMEM((2, ROWS, HEAD_SIZE), F32),
            pltpu.VMEM((2, HALF, HEAD_SIZE), F32),
            pltpu.VMEM((2, HALF, HEAD_SIZE), F32),
            pltpu.VMEM((HEAD_SIZE, ROWS), F32),
            full(HEADS),
            full(),
            full(),
            full(),
            full(),
            full(),
            full(),
            full(),
            dma((4,)),
            dma, dma, dma, dma, dma, dma, dma, dma, dma, dma,
            dma((HEADS,)), dma((HEADS,)),
            dma, dma, dma, dma, dma, dma, dma, dma, dma, dma,
        ],
        compiler_params=pltpu.CompilerParams(
            collective_id=1, has_side_effects=True, vmem_limit_bytes=48 << 20
        ),
        name="attention_backward",
    )(query_states, out_grad, attn_output, saved_key_rows, saved_value_rows, log_norm, block_pos)
    return qg, kvg[0], kvg[1]


def solution(mesh):
    tokens = P(("head", "ctx"), None)
    return jax.shard_map(
        shards,
        mesh=mesh,
        in_specs=(tokens,) * 6 + (P(),),
        out_specs=(tokens,) * 3,
        check_vma=False,
    )
```

```python
import jax
import jax.numpy as jnp
from jax import lax
from jax.experimental import pallas as pl
from jax.experimental.pallas import tpu as pltpu
from jax.sharding import PartitionSpec as P

HQ = 64
KEY_VALUE_HEADS = 8
HEAD_SIZE = 128
BLOCK = 64
N = 16
HEADS = HQ // N
ROWS = N * BLOCK
HALF = ROWS // 2
QUARTER = ROWS // 4
FACTOR = HEAD_SIZE**-0.5
LOG2E = 1.4426950408889634
MESH = pl.DeviceIdType.MESH
F32 = jnp.float32
BF16 = jnp.bfloat16


def dot(a, b):
    return jnp.dot(a, b, preferred_element_type=F32)


def dot_t(a, b):
    return lax.dot_general(a, b, (((1,), (1,)), ((), ())), preferred_element_type=F32)


def transposed(x):
    return x.astype(F32).T.astype(BF16)


def tile(k, kt, v, q, do, norm, delta, diagonal):
    s = dot_t(k, q)
    p = jnp.exp2(s * (FACTOR * LOG2E) - norm)
    if diagonal:
        key = lax.broadcasted_iota(jnp.int32, s.shape, 0)
        query = lax.broadcasted_iota(jnp.int32, s.shape, 1)
        p = jnp.where(query >= key, p, 0.0)
    ds = (p * (dot_t(v, do) - delta)).astype(BF16)
    return dot(kt, ds), dot(ds, q), dot(p.astype(BF16), do)


def kernel(
    q, do, at, k, v, log_norm, block_pos,
    qg, kvg,
    ln, bp, dov, atv, kvs, st_s, st_r, srow, qd, own, prev, own_t, prev_t, sel, sel_t,
    acc_own, acc_prev, acc_sel, dq_t, dq_s, x_s, x_r, ctx_s, ctx_r, y_s, y_r, fin,
    s_load, s_kv, r_kv, s_fw, r_fw, s_ctx, r_ctx, s_fwp, r_fwp, s_st, r_st, s_qd, r_qd,
    s_x, r_x, s_back, r_back, s_y, r_y, s_dq, r_dq, s_fin, r_fin,
):
    h = lax.axis_index("head")
    c = lax.axis_index("ctx")
    shift = lax.div(c, N // 2) * (N // 2)
    mine = lax.rem(h + shift, N)
    g = lax.div(mine, 2)
    m = lax.rem(h, 2)
    mate = h + 1 - 2 * m
    after = lax.rem(c + 1, N)
    before = lax.rem(c + N - 1, N)
    h_after = lax.rem(h + lax.div(lax.rem(c, N // 2) + 1, N // 2) * (N // 2), N)
    h_before = lax.rem(h + lax.div(lax.rem(before, N // 2) + 1, N // 2) * (N // 2), N)

    def remote(src, dst, ssem, rsem, **where):
        return pltpu.make_async_remote_copy(
            src_ref=src, dst_ref=dst, send_sem=ssem, recv_sem=rsem, device_id=where, device_id_type=MESH
        )

    def wait(ref, sem):
        pltpu.make_async_copy(ref, ref, sem).wait()

    def cols(j):
        return pl.ds(pl.multiple_of(j * HEAD_SIZE, HEAD_SIZE), HEAD_SIZE)

    def rows(j):
        return pl.ds(pl.multiple_of(j * BLOCK, BLOCK), BLOCK)

    loads = [
        pltpu.make_async_copy(k, kvs.at[0], s_load.at[0]),
        pltpu.make_async_copy(v, kvs.at[1], s_load.at[1]),
        pltpu.make_async_copy(do, dov, s_load.at[2]),
        pltpu.make_async_copy(at, atv, s_load.at[3]),
        pltpu.make_async_copy(log_norm, ln, s_load.at[4]),
        pltpu.make_async_copy(block_pos, bp, s_load.at[5]),
    ]
    for copy in loads:
        copy.start()

    barrier = pltpu.get_barrier_semaphore()

    @pl.loop(1, N)
    def _(s):
        pl.semaphore_signal(barrier, inc=1, device_id={"head": lax.rem(h + s, N)}, device_id_type=MESH)

    pl.semaphore_signal(barrier, inc=1, device_id={"head": h_after, "ctx": after}, device_id_type=MESH)
    pl.semaphore_signal(barrier, inc=1, device_id={"head": h_before, "ctx": before}, device_id_type=MESH)
    loads[0].wait()
    loads[1].wait()
    pl.semaphore_wait(barrier, N + 1)

    @pl.loop(1, N)
    def _(s):
        d = lax.rem(h + s, N)
        e = lax.rem(d, 2)
        remote(kvs.at[e, :, cols(lax.div(lax.rem(d + shift, N), 2))], own.at[e, rows(h)], s_kv, r_kv, head=d).start()

    pltpu.make_async_copy(kvs.at[m, :, cols(g)], own.at[m, rows(h)], r_kv).start()

    def send_head(i):
        @pl.loop(1, N)
        def _(s):
            d = lax.rem(h + s, N)
            for which, ref in ((0, q), (1, do)):
                remote(
                    ref.at[:, cols(lax.rem(d + shift, N) * HEADS + i)], qd.at[i, which, rows(h)], s_qd.at[i], r_qd.at[i], head=d
                ).start()

        for which, ref in ((0, q), (1, do)):
            pltpu.make_async_copy(ref.at[:, cols(mine * HEADS + i)], qd.at[i, which, rows(h)], r_qd.at[i]).start()

    send_head(0)

    for copy in loads[2:]:
        copy.wait()
    lane = lax.broadcasted_iota(jnp.int32, (BLOCK, 2 * BLOCK), 1)

    def inner(j, total):
        part = jnp.sum(dov[:, cols(j)].astype(F32) * atv[:, cols(j)].astype(F32), axis=1, keepdims=True)
        return jnp.where(lane == j, part, total)

    deltas = lax.fori_loop(0, HQ, inner, jnp.zeros((BLOCK, 2 * BLOCK), F32), unroll=8)
    stats = jnp.where(lane < BLOCK, deltas, jnp.concatenate([ln[...], ln[...]], axis=1) * LOG2E).T
    stats = jnp.concatenate([stats, stats], axis=1)
    for d in range(N):
        st_s[d, 0:HEADS] = stats[HQ + d * HEADS : HQ + (d + 1) * HEADS]
        st_s[d, HEADS:] = stats[d * HEADS : (d + 1) * HEADS]

    @pl.loop(1, N)
    def _(s):
        d = lax.rem(h + s, N)
        remote(st_s.at[lax.rem(d + shift, N)], st_r.at[h], s_st, r_st, head=d).start()

    pltpu.make_async_copy(st_s.at[mine], st_r.at[h], r_st).start()

    @pl.loop(1, HEADS)
    def _(i):
        send_head(i)

    wait(own.at[0], r_kv)
    forward = remote(own.at[m], own.at[m], s_fw, r_fw, head=mate)
    forward.start()
    onward = remote(own.at[m], prev.at[m], s_ctx, r_ctx, head=h_after, ctx=after)
    onward.start()
    forward.wait_recv()
    own_t[...] = transposed(own[0])

    wait(st_r, r_st)
    wide = lax.broadcasted_iota(jnp.int32, (2 * HEADS, 2 * BLOCK), 1)
    for pair in range(N // 2):
        srow[:, pair * 128 : (pair + 1) * 128] = jnp.where(wide < BLOCK, st_r[2 * pair], st_r[2 * pair + 1])

    onward.wait_recv()
    forward_prev = remote(prev.at[m], prev.at[m], s_fwp, r_fwp, head=mate)
    forward_prev.start()
    acc_own[...] = jnp.zeros_like(acc_own)
    acc_prev[...] = jnp.zeros_like(acc_prev)
    acc_sel[...] = jnp.zeros_like(acc_sel)
    forward_prev.wait_recv()

    early = bp[c] > bp[before]
    for which in range(2):
        sel[which] = jnp.where(early, prev[which, :HALF], prev[which, HALF:])
    prev_t[...] = transposed(prev[0, :HALF])
    sel_t[...] = transposed(sel[0])

    def add(ref, lo, size, dk, dv):
        ref[0, lo : lo + size] += dk
        ref[1, lo : lo + size] += dv

    def row(i, lo, size):
        return srow[pl.ds(i, 1), lo : lo + size], srow[pl.ds(HEADS + i, 1), lo : lo + size]

    def combined(which):
        chosen = acc_sel[which]
        zero = jnp.zeros_like(chosen)
        low = acc_prev[which] + jnp.where(early, chosen, zero)
        return low, jnp.where(early, zero, chosen)

    @pl.loop(0, HEADS)
    def _(i):
        wait(qd.at[i], r_qd.at[i])
        q_sel = jnp.where(early, qd[i, 0, :HALF], qd[i, 0, HALF:])
        do_sel = jnp.where(early, qd[i, 1, :HALF], qd[i, 1, HALF:])
        n0, d0 = row(i, 0, HALF)
        n1, d1 = row(i, HALF, HALF)
        dq, dk, dv = tile(
            sel[0], sel_t[...], sel[1], q_sel, do_sel, jnp.where(early, n0, n1), jnp.where(early, d0, d1), False
        )
        add(acc_sel, 0, HALF, dk, dv)
        zero = jnp.zeros_like(dq)
        dq_t[:, :HALF] = jnp.where(early, dq, zero)
        dq_t[:, HALF:] = jnp.where(early, zero, dq)
        dq, dk, dv = tile(
            prev[0, :HALF], prev_t[...], prev[1, :HALF], qd[i, 0, HALF:], qd[i, 1, HALF:], n1, d1, False
        )
        add(acc_prev, 0, HALF, dk, dv)
        dq_t[:, HALF:] += dq

        @pl.when(i == HEADS - 1)
        def _():
            low, high = combined(1 - m)
            x_s[:HALF] = low.astype(BF16)
            x_s[HALF:] = high.astype(BF16)
            remote(x_s, x_r, s_x, r_x, head=mate).start()

        dq, dk, dv = tile(
            own[0, :HALF], own_t[:, :HALF], own[1, :HALF], qd[i, 0, HALF:], qd[i, 1, HALF:], n1, d1, False
        )
        add(acc_own, 0, HALF, dk, dv)
        dq_t[:, HALF:] += dq

        @pl.when(i == HEADS - 1)
        def _():
            wait(x_r, r_x)
            low, high = combined(m)
            scale = jnp.where(m == 0, FACTOR, 1.0)
            ctx_s[:HALF] = ((low + x_r[:HALF].astype(F32)) * scale).astype(BF16)
            ctx_s[HALF:] = ((high + x_r[HALF:].astype(F32)) * scale).astype(BF16)
            remote(ctx_s, ctx_r, s_back, r_back, head=h_before, ctx=before).start()

        for kb, qb, size in ((0, 0, 1), (0, 1, 1), (1, 1, 1), (2, 2, 1), (2, 3, 1), (3, 3, 1)):
            ks = slice(kb * QUARTER, (kb + size) * QUARTER)
            qs = slice(qb * QUARTER, (qb + size) * QUARTER)
            nn, dd = row(i, qb * QUARTER, QUARTER)
            dq, dk, dv = tile(own[0, ks], own_t[:, ks], own[1, ks], qd[i, 0, qs], qd[i, 1, qs], nn, dd, kb == qb)
            add(acc_own, kb * QUARTER, QUARTER, dk, dv)
            dq_t[:, qs] += dq

        dq_s[i] = (dq_t[...] * FACTOR).T.astype(BF16)

        @pl.loop(1, N)
        def _(s):
            d = lax.rem(h + s, N)
            remote(dq_s.at[i, rows(d)], qg.at[:, cols(mine * HEADS + i)], s_dq, r_dq, head=d).start()

        pltpu.make_async_copy(dq_s.at[i, rows(h)], qg.at[:, cols(mine * HEADS + i)], r_dq).start()

    y_s[...] = acc_own[1 - m].astype(BF16)
    remote(y_s, y_r, s_y, r_y, head=mate).start()
    wait(y_r, r_y)
    wait(ctx_r, r_back)
    scale = jnp.where(m == 0, FACTOR, 1.0)
    fin[...] = ((acc_own[m] + y_r[...].astype(F32)) * scale + ctx_r[...].astype(F32)).astype(BF16)

    @pl.loop(1, N)
    def _(s):
        d = lax.rem(h + s, N)
        remote(fin.at[rows(d)], kvg.at[m, :, cols(g)], s_fin, r_fin, head=d).start()

    pltpu.make_async_copy(fin.at[rows(h)], kvg.at[m, :, cols(g)], r_fin).start()

    most = (N - 1) * BLOCK
    wait(own.at[0, :most], s_kv)
    forward.wait_send()
    onward.wait_send()
    forward_prev.wait_send()
    wait(st_r.at[: N - 1], s_st)
    for i in range(HEADS):
        wait(qd.at[i, :, :most], s_qd.at[i])
    wait(x_s, s_x)
    wait(ctx_s, s_back)
    wait(y_s, s_y)
    wait(dq_s.at[:, :most], s_dq)
    wait(fin.at[:most], s_fin)
    wait(qg, r_dq)
    wait(kvg, r_fin)


def shards(query_states, saved_key_rows, saved_value_rows, attn_output, out_grad, log_norm, block_pos):
    hbm = pl.BlockSpec(memory_space=pltpu.HBM)
    vmem = pl.BlockSpec(memory_space=pltpu.VMEM)
    inputs = (query_states, out_grad, attn_output, saved_key_rows, saved_value_rows, log_norm, block_pos)
    inputs = tuple(pltpu.with_memory_space_constraint(x, pltpu.HBM) for x in inputs)
    dma = pltpu.SemaphoreType.DMA
    half = lambda *lead: pltpu.VMEM((*lead, HALF, HEAD_SIZE), BF16)
    full = lambda *lead: pltpu.VMEM((*lead, ROWS, HEAD_SIZE), BF16)
    qg, kvg = pl.pallas_call(
        kernel,
        out_shape=(
            pltpu.VMEM((BLOCK, HQ * HEAD_SIZE), BF16),
            pltpu.VMEM((2, BLOCK, KEY_VALUE_HEADS * HEAD_SIZE), BF16),
        ),
        in_specs=[hbm] * 7,
        out_specs=(vmem, vmem),
        scratch_shapes=[
            pltpu.VMEM((BLOCK, HQ), F32),
            pltpu.SMEM((N * N,), jnp.int32),
            pltpu.VMEM((BLOCK, HQ * HEAD_SIZE), BF16),
            pltpu.VMEM((BLOCK, HQ * HEAD_SIZE), BF16),
            pltpu.VMEM((2, BLOCK, KEY_VALUE_HEADS * HEAD_SIZE), BF16),
            pltpu.VMEM((N, 2 * HEADS, 2 * BLOCK), F32),
            pltpu.VMEM((N, 2 * HEADS, 2 * BLOCK), F32),
            pltpu.VMEM((2 * HEADS, ROWS), F32),
            full(HEADS, 2),
            full(2),
            full(2),
            pltpu.VMEM((HEAD_SIZE, ROWS), BF16),
            pltpu.VMEM((HEAD_SIZE, HALF), BF16),
            half(2),
            pltpu.VMEM((HEAD_SIZE, HALF), BF16),
            pltpu.VMEM((2, ROWS, HEAD_SIZE), F32),
            pltpu.VMEM((2, HALF, HEAD_SIZE), F32),
            pltpu.VMEM((2, HALF, HEAD_SIZE), F32),
            pltpu.VMEM((HEAD_SIZE, ROWS), F32),
            full(HEADS),
            full(),
            full(),
            full(),
            full(),
            full(),
            full(),
            full(),
            dma((6,)),
            dma, dma, dma, dma, dma, dma, dma, dma, dma, dma,
            dma((HEADS,)), dma((HEADS,)),
            dma, dma, dma, dma, dma, dma, dma, dma, dma, dma,
        ],
        compiler_params=pltpu.CompilerParams(
            collective_id=1, has_side_effects=True, vmem_limit_bytes=48 << 20
        ),
        name="attention_backward",
    )(*inputs)
    return qg, kvg[0], kvg[1]


def solution(mesh):
    tokens = P(("head", "ctx"), None)
    return jax.shard_map(
        shards,
        mesh=mesh,
        in_specs=(tokens,) * 6 + (P(),),
        out_specs=(tokens,) * 3,
        check_vma=False,
    )
```

```python
import jax
import jax.numpy as jnp
from jax import lax
from jax.experimental import pallas as pl
from jax.experimental.pallas import tpu as pltpu
from jax.sharding import PartitionSpec as P

HQ = 64
KEY_VALUE_HEADS = 8
HEAD_SIZE = 128
BLOCK = 64
N = 16
HEADS = HQ // N
ROWS = N * BLOCK
HALF = ROWS // 2
QUARTER = ROWS // 4
PIECES = 4
FACTOR = HEAD_SIZE**-0.5
LOG2E = 1.4426950408889634
MESH = pl.DeviceIdType.MESH
F32 = jnp.float32
BF16 = jnp.bfloat16


def dot(a, b):
    return jnp.dot(a, b, preferred_element_type=F32)


def dot_t(a, b):
    return lax.dot_general(a, b, (((1,), (1,)), ((), ())), preferred_element_type=F32)


def transposed(x):
    return x.astype(F32).T.astype(BF16)


def scores(k, v, q, do):
    return dot_t(k, q), dot_t(v, do)


def terms(front, kt, q, do, norm, delta, diagonal):
    s, dp = front
    p = jnp.exp2(s * (FACTOR * LOG2E) - norm)
    if diagonal:
        key = lax.broadcasted_iota(jnp.int32, s.shape, 0)
        query = lax.broadcasted_iota(jnp.int32, s.shape, 1)
        p = jnp.where(query >= key, p, 0.0)
    ds = (p * (dp - delta)).astype(BF16)
    p = p.astype(BF16)
    dv = dot(p, do)
    dk = dot(ds, q)
    return dot(kt, ds), dk, dv


def in_turn(tiles):
    ahead = scores(*tiles[0][0])
    for n, (_, rest, keep) in enumerate(tiles):
        front = ahead
        if n + 1 < len(tiles):
            ahead = scores(*tiles[n + 1][0])
        keep(*terms(front, *rest))


def kernel(
    q, do, at, k, v, log_norm, block_pos,
    qg, kvg,
    ln, bp, dov, atv, kvs, st_s, st_r, srow, qd, own, prev, own_t, prev_t, sel, sel_t,
    acc_own, acc_prev, acc_sel, dq_t, dq_s, x_s, x_r, ctx_s, ctx_r, y_s, y_r, fin,
    s_load, s_kv, r_kv, s_fw, r_fw, s_ctx, r_ctx, s_fwp, r_fwp, s_st, r_st, s_qd, r_qd,
    s_x, r_x, s_back, r_back, s_y, r_y, s_dq, r_dq, s_fin, r_fin,
):
    h = lax.axis_index("head")
    c = lax.axis_index("ctx")
    shift = lax.div(c, N // 2) * (N // 2)
    mine = lax.rem(h + shift, N)
    g = lax.div(mine, 2)
    m = lax.rem(h, 2)
    mate = h + 1 - 2 * m
    after = lax.rem(c + 1, N)
    before = lax.rem(c + N - 1, N)
    h_after = lax.rem(h + lax.div(lax.rem(c, N // 2) + 1, N // 2) * (N // 2), N)
    h_before = lax.rem(h + lax.div(lax.rem(before, N // 2) + 1, N // 2) * (N // 2), N)

    def remote(src, dst, ssem, rsem, **where):
        return pltpu.make_async_remote_copy(
            src_ref=src, dst_ref=dst, send_sem=ssem, recv_sem=rsem, device_id=where, device_id_type=MESH
        )

    def wait(ref, sem):
        pltpu.make_async_copy(ref, ref, sem).wait()

    def cols(j):
        return pl.ds(pl.multiple_of(j * HEAD_SIZE, HEAD_SIZE), HEAD_SIZE)

    def rows(j):
        return pl.ds(pl.multiple_of(j * BLOCK, BLOCK), BLOCK)

    loads = [
        pltpu.make_async_copy(k, kvs.at[0], s_load.at[0]),
        pltpu.make_async_copy(v, kvs.at[1], s_load.at[1]),
        pltpu.make_async_copy(do, dov, s_load.at[2]),
        pltpu.make_async_copy(at, atv, s_load.at[3]),
        pltpu.make_async_copy(log_norm, ln, s_load.at[4]),
        pltpu.make_async_copy(block_pos, bp, s_load.at[5]),
    ]
    for copy in loads:
        copy.start()

    barrier = pltpu.get_barrier_semaphore()

    @pl.loop(1, N)
    def _(s):
        pl.semaphore_signal(barrier, inc=1, device_id={"head": lax.rem(h + s, N)}, device_id_type=MESH)

    pl.semaphore_signal(barrier, inc=1, device_id={"head": h_before, "ctx": before}, device_id_type=MESH)
    loads[0].wait()
    loads[1].wait()
    pl.semaphore_wait(barrier, N)

    @pl.loop(1, N)
    def _(s):
        d = lax.rem(h + s, N)
        e = lax.rem(d, 2)
        remote(kvs.at[e, :, cols(lax.div(lax.rem(d + shift, N), 2))], own.at[e, rows(h)], s_kv, r_kv, head=d).start()

    pltpu.make_async_copy(kvs.at[m, :, cols(g)], own.at[m, rows(h)], r_kv).start()

    def send_head(i):
        @pl.loop(1, N)
        def _(s):
            d = lax.rem(h + s, N)
            for which, ref in ((0, q), (1, do)):
                remote(
                    ref.at[:, cols(lax.rem(d + shift, N) * HEADS + i)], qd.at[i, which, rows(h)], s_qd.at[i], r_qd.at[i], head=d
                ).start()

        for which, ref in ((0, q), (1, do)):
            pltpu.make_async_copy(ref.at[:, cols(mine * HEADS + i)], qd.at[i, which, rows(h)], r_qd.at[i]).start()

    send_head(0)

    for copy in loads[2:]:
        copy.wait()
    lane = lax.broadcasted_iota(jnp.int32, (BLOCK, 2 * BLOCK), 1)

    def inner(j, total):
        part = jnp.sum(dov[:, cols(j)].astype(F32) * atv[:, cols(j)].astype(F32), axis=1, keepdims=True)
        return jnp.where(lane == j, part, total)

    deltas = lax.fori_loop(0, HQ, inner, jnp.zeros((BLOCK, 2 * BLOCK), F32), unroll=8)
    stats = jnp.where(lane < BLOCK, deltas, jnp.concatenate([ln[...], ln[...]], axis=1) * LOG2E).T
    stats = jnp.concatenate([stats[:HQ], stats[HQ:]], axis=1)
    for d in range(N):
        st_s[d] = stats[d * HEADS : (d + 1) * HEADS]

    @pl.loop(1, N)
    def _(s):
        d = lax.rem(h + s, N)
        remote(st_s.at[lax.rem(d + shift, N)], st_r.at[h], s_st, r_st, head=d).start()

    pltpu.make_async_copy(st_s.at[mine], st_r.at[h], r_st).start()

    wait(own.at[0], r_kv)
    forward = remote(own.at[m], own.at[m], s_fw, r_fw, head=mate)
    forward.start()
    onward = remote(own.at[m], prev.at[m], s_ctx, r_ctx, head=h_after, ctx=after)
    onward.start()

    @pl.loop(1, HEADS)
    def _(i):
        send_head(i)

    forward.wait_recv()
    own_t[...] = transposed(own[0])

    wait(st_r, r_st)
    for pair in range(N // 2):
        a, b = st_r[2 * pair], st_r[2 * pair + 1]
        at_pair = slice(pair * 2 * BLOCK, (pair + 1) * 2 * BLOCK)
        srow[:HEADS, at_pair] = jnp.concatenate([a[:, BLOCK:], b[:, BLOCK:]], axis=1)
        srow[HEADS:, at_pair] = jnp.concatenate([a[:, :BLOCK], b[:, :BLOCK]], axis=1)

    acc_own[...] = jnp.zeros_like(acc_own)
    acc_prev[...] = jnp.zeros_like(acc_prev)
    acc_sel[...] = jnp.zeros_like(acc_sel)
    dq_t[...] = jnp.zeros_like(dq_t)
    early = bp[c] > bp[before]

    def take_prev():
        onward.wait_recv()
        copy = remote(prev.at[m], prev.at[m], s_fwp, r_fwp, head=mate)
        copy.start()
        copy.wait_recv()
        for which in range(2):
            sel[which] = jnp.where(early, prev[which, :HALF], prev[which, HALF:])
        prev_t[...] = transposed(prev[0, :HALF])
        sel_t[...] = transposed(sel[0])

    def add(ref, lo, size, dk, dv):
        ref[0, lo : lo + size] += dk
        ref[1, lo : lo + size] += dv

    def pieces(x):
        return x.reshape(-1, PIECES, BLOCK, HEAD_SIZE)

    def row(i, lo, size):
        return srow[pl.ds(i, 1), lo : lo + size], srow[pl.ds(HEADS + i, 1), lo : lo + size]

    def combined(which):
        chosen = acc_sel[which]
        zero = jnp.zeros_like(chosen)
        low = acc_prev[which] + jnp.where(early, chosen, zero)
        return low, jnp.where(early, zero, chosen)

    def other_group(i):
        n0, d0 = row(i, 0, HALF)
        n1, d1 = row(i, HALF, HALF)
        q_sel = jnp.where(early, qd[i, 0, :HALF], qd[i, 0, HALF:])
        do_sel = jnp.where(early, qd[i, 1, :HALF], qd[i, 1, HALF:])
        n_sel, d_sel = jnp.where(early, n0, n1), jnp.where(early, d0, d1)
        q1, do1 = qd[i, 0, HALF:], qd[i, 1, HALF:]

        def keep_sel(dq, dk, dv):
            add(acc_sel, 0, HALF, dk, dv)
            zero = jnp.zeros_like(dq)
            dq_t[i, :, :HALF] += jnp.where(early, dq, zero)
            dq_t[i, :, HALF:] += jnp.where(early, zero, dq)

        def keep_prev(dq, dk, dv):
            add(acc_prev, 0, HALF, dk, dv)
            dq_t[i, :, HALF:] += dq

        in_turn([
            ((sel[0], sel[1], q_sel, do_sel), (sel_t[...], q_sel, do_sel, n_sel, d_sel, False), keep_sel),
            ((prev[0, :HALF], prev[1, :HALF], q1, do1), (prev_t[...], q1, do1, n1, d1, False), keep_prev),
        ])

    def own_tile(i, k0, k1, q0, q1, diagonal):
        q, do = qd[i, 0, q0:q1], qd[i, 1, q0:q1]
        norm, delta = row(i, q0, q1 - q0)

        def keep(dq, dk, dv):
            add(acc_own, k0, k1 - k0, dk, dv)
            dq_t[i, :, q0:q1] += dq

        return (own[0, k0:k1], own[1, k0:k1], q, do), (own_t[:, k0:k1], q, do, norm, delta, diagonal), keep

    def own_group(i, between):
        in_turn([own_tile(i, 0, HALF, HALF, ROWS, False)])
        between()
        in_turn([
            own_tile(i, 0, QUARTER, 0, HALF, True),
            own_tile(i, QUARTER, HALF, QUARTER, HALF, True),
            own_tile(i, HALF, HALF + QUARTER, HALF, ROWS, True),
            own_tile(i, HALF + QUARTER, ROWS, HALF + QUARTER, ROWS, True),
        ])

    @pl.loop(0, 2 * HEADS)
    def _(t):
        i = jnp.where(t < 4, lax.rem(t, 2), lax.div(t, 2))
        first = (t < 2) | (t == 4) | (t == 6)
        is_own = (t < 2) | (t == 4) | (t == 7)

        @pl.when(first)
        def _():
            wait(qd.at[i], r_qd.at[i])

        @pl.when(t == 2)
        def _():
            take_prev()

        @pl.when(jnp.logical_not(is_own))
        def _():
            other_group(i)

        @pl.when(t == 6)
        def _():
            low, high = combined(1 - m)
            x_s[:HALF] = low.astype(BF16)
            x_s[HALF:] = high.astype(BF16)
            remote(x_s, x_r, s_x, r_x, head=mate).start()

        def send_back():
            @pl.when(t == 7)
            def _():
                wait(x_r, r_x)
                low, high = combined(m)
                scale = jnp.where(m == 0, FACTOR, 1.0)
                low = pieces(((low + x_r[:HALF].astype(F32)) * scale).astype(BF16))
                high = pieces(((high + x_r[HALF:].astype(F32)) * scale).astype(BF16))
                for e in range(PIECES):
                    ctx_s[: N // PIECES // 2, e] = low[:, e]
                    ctx_s[N // PIECES // 2 :, e] = high[:, e]
                    remote(
                        ctx_s.at[:, e], ctx_r.at[:, e], s_back.at[e], r_back.at[e], head=h_before, ctx=before
                    ).start()

        @pl.when(is_own)
        def _():
            own_group(i, send_back)

        @pl.when(jnp.logical_not(first))
        def _():
            dq_s[i] = (dq_t[i] * FACTOR).T.astype(BF16)

            @pl.loop(1, N)
            def _(s):
                d = lax.rem(h + s, N)
                remote(dq_s.at[i, rows(d)], qg.at[:, cols(mine * HEADS + i)], s_dq, r_dq, head=d).start()

            pltpu.make_async_copy(dq_s.at[i, rows(h)], qg.at[:, cols(mine * HEADS + i)], r_dq).start()

    y_s[...] = acc_own[1 - m].astype(BF16)
    remote(y_s, y_r, s_y, r_y, head=mate).start()
    scale = jnp.where(m == 0, FACTOR, 1.0)
    wait(y_r, r_y)
    total = pieces((acc_own[m] + y_r[...].astype(F32)) * scale)
    for e in range(PIECES):
        wait(ctx_r.at[:, e], r_back.at[e])
        fin[:, e] = (total[:, e] + ctx_r[:, e].astype(F32)).astype(BF16)

        @pl.loop(0, N // PIECES)
        def _(s):
            t = lax.rem(lax.div(h, PIECES) + s, N // PIECES)
            d = t * PIECES + e

            @pl.when(d != h)
            def _():
                remote(fin.at[t, e], kvg.at[m, :, cols(g)], s_fin, r_fin, head=d).start()

            @pl.when(d == h)
            def _():
                pltpu.make_async_copy(fin.at[t, e], kvg.at[m, :, cols(g)], r_fin).start()

    most = (N - 1) * BLOCK
    wait(own.at[0, :most], s_kv)
    forward.wait_send()
    onward.wait_send()
    wait(prev.at[0], s_fwp)
    wait(st_r.at[: N - 1], s_st)
    for i in range(HEADS):
        wait(qd.at[i, :, :most], s_qd.at[i])
    wait(x_s, s_x)
    for e in range(PIECES):
        wait(ctx_s.at[:, e], s_back.at[e])
    wait(y_s, s_y)
    wait(dq_s.at[:, :most], s_dq)
    wait(own.at[0, :most], s_fin)
    wait(qg, r_dq)
    wait(kvg, r_fin)


def flush(qg, kvg, query_grad, key_gradient, value_gradient, sem):
    copies = [
        pltpu.make_async_copy(qg, query_grad, sem.at[0]),
        pltpu.make_async_copy(kvg.at[0], key_gradient, sem.at[1]),
        pltpu.make_async_copy(kvg.at[1], value_gradient, sem.at[2]),
    ]
    for copy in copies:
        copy.start()
    for copy in copies:
        copy.wait()


def shards(query_states, saved_key_rows, saved_value_rows, attn_output, out_grad, log_norm, block_pos):
    hbm = pl.BlockSpec(memory_space=pltpu.HBM)
    vmem = pl.BlockSpec(memory_space=pltpu.VMEM)
    inputs = (query_states, out_grad, attn_output, saved_key_rows, saved_value_rows, log_norm, block_pos)
    inputs = tuple(pltpu.with_memory_space_constraint(x, pltpu.HBM) for x in inputs)
    dma = pltpu.SemaphoreType.DMA
    half = lambda *lead: pltpu.VMEM((*lead, HALF, HEAD_SIZE), BF16)
    parts = pltpu.VMEM((N // PIECES, PIECES, BLOCK, HEAD_SIZE), BF16)
    full = lambda *lead: pltpu.VMEM((*lead, ROWS, HEAD_SIZE), BF16)
    qg, kvg = pl.pallas_call(
        kernel,
        out_shape=(
            pltpu.VMEM((BLOCK, HQ * HEAD_SIZE), BF16),
            pltpu.VMEM((2, BLOCK, KEY_VALUE_HEADS * HEAD_SIZE), BF16),
        ),
        in_specs=[hbm] * 7,
        out_specs=(vmem, vmem),
        scratch_shapes=[
            pltpu.VMEM((BLOCK, HQ), F32),
            pltpu.SMEM((N * N,), jnp.int32),
            pltpu.VMEM((BLOCK, HQ * HEAD_SIZE), BF16),
            pltpu.VMEM((BLOCK, HQ * HEAD_SIZE), BF16),
            pltpu.VMEM((2, BLOCK, KEY_VALUE_HEADS * HEAD_SIZE), BF16),
            pltpu.VMEM((N, HEADS, 2 * BLOCK), F32),
            pltpu.VMEM((N, HEADS, 2 * BLOCK), F32),
            pltpu.VMEM((2 * HEADS, ROWS), F32),
            full(HEADS, 2),
            full(2),
            full(2),
            pltpu.VMEM((HEAD_SIZE, ROWS), BF16),
            pltpu.VMEM((HEAD_SIZE, HALF), BF16),
            half(2),
            pltpu.VMEM((HEAD_SIZE, HALF), BF16),
            pltpu.VMEM((2, ROWS, HEAD_SIZE), F32),
            pltpu.VMEM((2, HALF, HEAD_SIZE), F32),
            pltpu.VMEM((2, HALF, HEAD_SIZE), F32),
            pltpu.VMEM((HEADS, HEAD_SIZE, ROWS), F32),
            full(HEADS),
            full(),
            full(),
            parts,
            parts,
            full(),
            full(),
            parts,
            dma((6,)),
            dma, dma, dma, dma, dma, dma, dma, dma, dma, dma,
            dma((HEADS,)), dma((HEADS,)),
            dma, dma, dma((PIECES,)), dma((PIECES,)), dma, dma, dma, dma, dma, dma,
        ],
        compiler_params=pltpu.CompilerParams(
            collective_id=1, has_side_effects=True, vmem_limit_bytes=48 << 20
        ),
        name="attention_backward",
    )(*inputs)
    return pl.pallas_call(
        flush,
        out_shape=(
            pltpu.HBM((BLOCK, HQ * HEAD_SIZE), BF16),
            pltpu.HBM((BLOCK, KEY_VALUE_HEADS * HEAD_SIZE), BF16),
            pltpu.HBM((BLOCK, KEY_VALUE_HEADS * HEAD_SIZE), BF16),
        ),
        in_specs=[vmem] * 2,
        out_specs=(hbm,) * 3,
        scratch_shapes=[dma((3,))],
        name="store_results",
    )(*(pltpu.with_memory_space_constraint(x, pltpu.VMEM) for x in (qg, kvg)))


def solution(mesh):
    tokens = P(("head", "ctx"), None)
    return jax.shard_map(
        shards,
        mesh=mesh,
        in_specs=(tokens,) * 6 + (P(),),
        out_specs=(tokens,) * 3,
        check_vma=False,
    )
```

```python
import jax
import jax.numpy as jnp
from jax import lax
from jax.experimental import pallas as pl
from jax.experimental.pallas import tpu as pltpu
from jax.sharding import PartitionSpec as P

HQ = 64
KEY_VALUE_HEADS = 8
HEAD_SIZE = 128
BLOCK = 64
N = 16
HEADS = HQ // N
ROWS = N * BLOCK
HALF = ROWS // 2
QUARTER = ROWS // 4
PIECES = 4
FACTOR = HEAD_SIZE**-0.5
LOG2E = 1.4426950408889634
MESH = pl.DeviceIdType.MESH
F32 = jnp.float32
BF16 = jnp.bfloat16


def dot(a, b):
    return jnp.dot(a, b, preferred_element_type=F32)


def dot_t(a, b):
    return lax.dot_general(a, b, (((1,), (1,)), ((), ())), preferred_element_type=F32)


def transposed(x):
    return x.T


def scores(k, v, q, do):
    return dot_t(k, q), dot_t(v, do)


def terms(front, kt, q, do, norm, delta, diagonal):
    s, dp = front
    p = jnp.exp2(s * (FACTOR * LOG2E) - norm)
    if diagonal:
        key = lax.broadcasted_iota(jnp.int32, s.shape, 0)
        query = lax.broadcasted_iota(jnp.int32, s.shape, 1)
        p = jnp.where(query >= key, p, 0.0)
    ds = (p * (dp - delta)).astype(BF16)
    p = p.astype(BF16)
    dv = dot(p, do)
    dk = dot(ds, q)
    return dot(kt, ds), dk, dv


def in_turn(tiles):
    ahead = scores(*tiles[0][0])
    for n, (_, rest, keep) in enumerate(tiles):
        front = ahead
        if n + 1 < len(tiles):
            ahead = scores(*tiles[n + 1][0])
        keep(*terms(front, *rest))


def kernel(
    q, do, at, k, v, log_norm, block_pos,
    qg, kvg,
    ln, bp, dov, atv, kvs, st_s, st_r, srow, qd, own, prev, own_t, prev_t, sel, sel_t,
    acc_own, acc_prev, acc_sel, dq_t, dq_s, x_s, x_r, back_s, back_r, ctx_s, ctx_r, y_s, y_r, fin,
    s_load, s_kv, r_kv, s_fw, r_fw, s_ctx, r_ctx, s_fwp, r_fwp, s_st, r_st, s_qd, r_qd,
    s_x, r_x, s_back, r_back, s_y, r_y, s_dq, r_dq, s_fin, r_fin,
):
    h = lax.axis_index("head")
    c = lax.axis_index("ctx")
    shift = lax.div(c, N // 2) * (N // 2)
    mine = lax.rem(h + shift, N)
    g = lax.div(mine, 2)
    m = lax.rem(h, 2)
    mate = h + 1 - 2 * m
    after = lax.rem(c + 1, N)
    before = lax.rem(c + N - 1, N)
    h_after = lax.rem(h + lax.div(lax.rem(c, N // 2) + 1, N // 2) * (N // 2), N)
    h_before = lax.rem(h + lax.div(lax.rem(before, N // 2) + 1, N // 2) * (N // 2), N)

    def remote(src, dst, ssem, rsem, **where):
        return pltpu.make_async_remote_copy(
            src_ref=src, dst_ref=dst, send_sem=ssem, recv_sem=rsem, device_id=where, device_id_type=MESH
        )

    def wait(ref, sem):
        pltpu.make_async_copy(ref, ref, sem).wait()

    def cols(j):
        return pl.ds(pl.multiple_of(j * HEAD_SIZE, HEAD_SIZE), HEAD_SIZE)

    def rows(j):
        return pl.ds(pl.multiple_of(j * BLOCK, BLOCK), BLOCK)

    loads = [
        pltpu.make_async_copy(k, kvs.at[0], s_load.at[0]),
        pltpu.make_async_copy(v, kvs.at[1], s_load.at[1]),
        pltpu.make_async_copy(do, dov, s_load.at[2]),
        pltpu.make_async_copy(at, atv, s_load.at[3]),
        pltpu.make_async_copy(log_norm, ln, s_load.at[4]),
        pltpu.make_async_copy(block_pos, bp, s_load.at[5]),
    ]
    for copy in loads:
        copy.start()

    barrier = pltpu.get_barrier_semaphore()

    @pl.loop(1, N)
    def _(s):
        pl.semaphore_signal(barrier, inc=1, device_id={"head": lax.rem(h + s, N)}, device_id_type=MESH)

    pl.semaphore_signal(barrier, inc=1, device_id={"head": h_before, "ctx": before}, device_id_type=MESH)
    loads[0].wait()
    loads[1].wait()
    pl.semaphore_wait(barrier, N)

    @pl.loop(1, N)
    def _(s):
        d = lax.rem(h + s, N)
        e = lax.rem(d, 2)
        remote(kvs.at[e, :, cols(lax.div(lax.rem(d + shift, N), 2))], own.at[e, rows(h)], s_kv, r_kv, head=d).start()

    pltpu.make_async_copy(kvs.at[m, :, cols(g)], own.at[m, rows(h)], r_kv).start()

    def send_head(i):
        @pl.loop(1, N)
        def _(s):
            d = lax.rem(h + s, N)
            for which, ref in ((0, q), (1, do)):
                remote(
                    ref.at[:, cols(lax.rem(d + shift, N) * HEADS + i)], qd.at[i, which, rows(h)], s_qd.at[i], r_qd.at[i], head=d
                ).start()

        for which, ref in ((0, q), (1, do)):
            pltpu.make_async_copy(ref.at[:, cols(mine * HEADS + i)], qd.at[i, which, rows(h)], r_qd.at[i]).start()

    send_head(0)

    for copy in loads[2:]:
        copy.wait()
    lane = lax.broadcasted_iota(jnp.int32, (BLOCK, 2 * BLOCK), 1)

    def inner(j, total):
        part = jnp.sum(dov[:, cols(j)].astype(F32) * atv[:, cols(j)].astype(F32), axis=1, keepdims=True)
        return jnp.where(lane == j, part, total)

    deltas = lax.fori_loop(0, HQ, inner, jnp.zeros((BLOCK, 2 * BLOCK), F32), unroll=8)
    stats = jnp.where(lane < BLOCK, deltas, jnp.concatenate([ln[...], ln[...]], axis=1) * LOG2E).T
    stats = jnp.concatenate([stats[:HQ], stats[HQ:]], axis=1)
    for d in range(N):
        st_s[d] = stats[d * HEADS : (d + 1) * HEADS]

    @pl.loop(1, N)
    def _(s):
        d = lax.rem(h + s, N)
        remote(st_s.at[lax.rem(d + shift, N)], st_r.at[h], s_st, r_st, head=d).start()

    pltpu.make_async_copy(st_s.at[mine], st_r.at[h], r_st).start()

    wait(own.at[0], r_kv)
    forward = remote(own.at[m], own.at[m], s_fw, r_fw, head=mate)
    forward.start()
    onward = remote(own.at[m], prev.at[m], s_ctx, r_ctx, head=h_after, ctx=after)
    onward.start()

    @pl.loop(1, HEADS)
    def _(i):
        send_head(i)

    forward.wait_recv()
    own_t[...] = transposed(own[0])

    wait(st_r, r_st)
    for pair in range(N // 2):
        a, b = st_r[2 * pair], st_r[2 * pair + 1]
        at_pair = slice(pair * 2 * BLOCK, (pair + 1) * 2 * BLOCK)
        srow[:HEADS, at_pair] = jnp.concatenate([a[:, BLOCK:], b[:, BLOCK:]], axis=1)
        srow[HEADS:, at_pair] = jnp.concatenate([a[:, :BLOCK], b[:, :BLOCK]], axis=1)

    acc_own[...] = jnp.zeros_like(acc_own)
    acc_prev[...] = jnp.zeros_like(acc_prev)
    acc_sel[...] = jnp.zeros_like(acc_sel)
    dq_t[...] = jnp.zeros_like(dq_t)
    early = bp[c] > bp[before]

    def share_prev():
        return remote(prev.at[m], prev.at[m], s_fwp, r_fwp, head=mate)

    def take_prev():
        share_prev().wait_recv()
        for which in range(2):
            sel[which] = jnp.where(early, prev[which, :HALF], prev[which, HALF:])
        prev_t[...] = transposed(prev[0, :HALF])
        sel_t[...] = transposed(sel[0])

    def add(ref, lo, size, dk, dv):
        ref[0, lo : lo + size] += dk
        ref[1, lo : lo + size] += dv

    def pieces(x):
        return x.reshape(-1, PIECES, BLOCK, HEAD_SIZE)

    def row(i, lo, size):
        return srow[pl.ds(i, 1), lo : lo + size], srow[pl.ds(HEADS + i, 1), lo : lo + size]

    def swap(n):
        return remote(x_s.at[n], x_r.at[n], s_x.at[n], r_x.at[n], head=mate)

    def both_cores(ref, n):
        wait(x_r.at[n], r_x.at[n])
        scale = jnp.where(m == 0, FACTOR, 1.0)
        return ((ref[m] + x_r[n].astype(F32)) * scale).astype(BF16)

    def other_tiles(i):
        n0, d0 = row(i, 0, HALF)
        n1, d1 = row(i, HALF, HALF)
        q_sel = jnp.where(early, qd[i, 0, :HALF], qd[i, 0, HALF:])
        do_sel = jnp.where(early, qd[i, 1, :HALF], qd[i, 1, HALF:])
        n_sel, d_sel = jnp.where(early, n0, n1), jnp.where(early, d0, d1)
        q1, do1 = qd[i, 0, HALF:], qd[i, 1, HALF:]

        def keep_sel(dq, dk, dv):
            add(acc_sel, 0, HALF, dk, dv)
            zero = jnp.zeros_like(dq)
            dq_t[i, :, :HALF] += jnp.where(early, dq, zero)
            dq_t[i, :, HALF:] += jnp.where(early, zero, dq)

        def keep_prev(dq, dk, dv):
            add(acc_prev, 0, HALF, dk, dv)
            dq_t[i, :, HALF:] += dq

        return (
            ((prev[0, :HALF], prev[1, :HALF], q1, do1), (prev_t[...], q1, do1, n1, d1, False), keep_prev),
            ((sel[0], sel[1], q_sel, do_sel), (sel_t[...], q_sel, do_sel, n_sel, d_sel, False), keep_sel),
        )

    def own_tile(i, k0, k1, q0, q1, diagonal):
        q, do = qd[i, 0, q0:q1], qd[i, 1, q0:q1]
        norm, delta = row(i, q0, q1 - q0)

        def keep(dq, dk, dv):
            add(acc_own, k0, k1 - k0, dk, dv)
            dq_t[i, :, q0:q1] += dq

        return (own[0, k0:k1], own[1, k0:k1], q, do), (own_t[:, k0:k1], q, do, norm, delta, diagonal), keep

    def own_group(i):
        in_turn([
            own_tile(i, 0, HALF, HALF, ROWS, False),
            own_tile(i, 0, QUARTER, 0, HALF, True),
            own_tile(i, QUARTER, HALF, QUARTER, HALF, True),
            own_tile(i, HALF, HALF + QUARTER, HALF, ROWS, True),
            own_tile(i, HALF + QUARTER, ROWS, HALF + QUARTER, ROWS, True),
        ])

    def round_dq(i):
        dq_s[i] = (dq_t[i] * FACTOR).astype(BF16).T

    def send_dq(i):
        @pl.loop(1, N)
        def _(s):
            d = lax.rem(h + s, N)
            remote(dq_s.at[i, rows(d)], qg.at[:, cols(mine * HEADS + i)], s_dq, r_dq, head=d).start()

        pltpu.make_async_copy(dq_s.at[i, rows(h)], qg.at[:, cols(mine * HEADS + i)], r_dq).start()

    @pl.loop(0, 2 * HEADS)
    def _(t):
        i = jnp.where(t < 4, lax.rem(t, 2), lax.div(t, 2))
        first = (t < 2) | (t == 4) | (t == 6)
        is_own = (t < 2) | (t == 4) | (t == 7)

        @pl.when(first)
        def _():
            wait(qd.at[i], r_qd.at[i])

        @pl.when(t == 1)
        def _():
            onward.wait_recv()
            share_prev().start()

        @pl.when(t == 2)
        def _():
            take_prev()

        @pl.when(jnp.logical_not(is_own | (t == 6)))
        def _():
            in_turn(other_tiles(i))

        @pl.when(t == 6)
        def _():
            for n, (spec, ref) in enumerate(zip(other_tiles(i), (acc_prev, acc_sel))):
                in_turn([spec])
                x_s[n] = ref[1 - m].astype(BF16)
                swap(n).start()
            back_s[...] = both_cores(acc_prev, 0)
            remote(back_s, back_r, s_back.at[PIECES], r_back.at[PIECES], head=h_before, ctx=before).start()
            round_dq(i - 1)
            chosen = pieces(both_cores(acc_sel, 1))
            for e in range(PIECES):
                ctx_s[:, e] = chosen[:, e]
                remote(
                    ctx_s.at[:, e], ctx_r.at[:, e], s_back.at[e], r_back.at[e], head=h_before, ctx=before
                ).start()
            send_dq(i - 1)

        @pl.when(is_own)
        def _():
            own_group(i)

        @pl.when(jnp.logical_not(first | (t == 5)))
        def _():
            round_dq(i)
            send_dq(i)

    y_s[...] = acc_own[1 - m].astype(BF16)
    remote(y_s, y_r, s_y, r_y, head=mate).start()
    scale = jnp.where(m == 0, FACTOR, 1.0)
    wait(y_r, r_y)
    total = pieces((acc_own[m] + y_r[...].astype(F32)) * scale)
    next_early = bp[after] > bp[c]
    wait(back_r, r_back.at[PIECES])
    low = total[: N // PIECES // 2] + pieces(back_r[...]).astype(F32)
    high = total[N // PIECES // 2 :]
    for e in range(PIECES):
        wait(ctx_r.at[:, e], r_back.at[e])
        chosen = ctx_r[:, e].astype(F32)
        zero = jnp.zeros_like(chosen)
        fin[: N // PIECES // 2, e] = (low[:, e] + jnp.where(next_early, chosen, zero)).astype(BF16)
        fin[N // PIECES // 2 :, e] = (high[:, e] + jnp.where(next_early, zero, chosen)).astype(BF16)

        @pl.loop(0, N // PIECES)
        def _(s):
            t = lax.rem(lax.div(h, PIECES) + s, N // PIECES)
            d = t * PIECES + e

            @pl.when(d != h)
            def _():
                remote(fin.at[t, e], kvg.at[m, :, cols(g)], s_fin, r_fin, head=d).start()

            @pl.when(d == h)
            def _():
                pltpu.make_async_copy(fin.at[t, e], kvg.at[m, :, cols(g)], r_fin).start()

    most = (N - 1) * BLOCK
    wait(own.at[0, :most], s_kv)
    forward.wait_send()
    onward.wait_send()
    wait(prev.at[0], s_fwp)
    wait(st_r.at[: N - 1], s_st)
    for i in range(HEADS):
        wait(qd.at[i, :, :most], s_qd.at[i])
    for n in range(2):
        wait(x_s.at[n], s_x.at[n])
    wait(back_s, s_back.at[PIECES])
    for e in range(PIECES):
        wait(ctx_s.at[:, e], s_back.at[e])
    wait(y_s, s_y)
    wait(dq_s.at[:, :most], s_dq)
    wait(own.at[0, :most], s_fin)
    wait(qg, r_dq)
    wait(kvg, r_fin)


def flush(qg, kvg, query_grad, key_gradient, value_gradient, sem):
    copies = [
        pltpu.make_async_copy(qg, query_grad, sem.at[0]),
        pltpu.make_async_copy(kvg.at[0], key_gradient, sem.at[1]),
        pltpu.make_async_copy(kvg.at[1], value_gradient, sem.at[2]),
    ]
    for copy in copies:
        copy.start()
    for copy in copies:
        copy.wait()


def shards(query_states, saved_key_rows, saved_value_rows, attn_output, out_grad, log_norm, block_pos):
    hbm = pl.BlockSpec(memory_space=pltpu.HBM)
    vmem = pl.BlockSpec(memory_space=pltpu.VMEM)
    inputs = (query_states, out_grad, attn_output, saved_key_rows, saved_value_rows, log_norm, block_pos)
    inputs = tuple(pltpu.with_memory_space_constraint(x, pltpu.HBM) for x in inputs)
    dma = pltpu.SemaphoreType.DMA
    half = lambda *lead: pltpu.VMEM((*lead, HALF, HEAD_SIZE), BF16)
    parts = pltpu.VMEM((N // PIECES, PIECES, BLOCK, HEAD_SIZE), BF16)
    full = lambda *lead: pltpu.VMEM((*lead, ROWS, HEAD_SIZE), BF16)
    qg, kvg = pl.pallas_call(
        kernel,
        out_shape=(
            pltpu.VMEM((BLOCK, HQ * HEAD_SIZE), BF16),
            pltpu.VMEM((2, BLOCK, KEY_VALUE_HEADS * HEAD_SIZE), BF16),
        ),
        in_specs=[hbm] * 7,
        out_specs=(vmem, vmem),
        scratch_shapes=[
            pltpu.VMEM((BLOCK, HQ), F32),
            pltpu.SMEM((N * N,), jnp.int32),
            pltpu.VMEM((BLOCK, HQ * HEAD_SIZE), BF16),
            pltpu.VMEM((BLOCK, HQ * HEAD_SIZE), BF16),
            pltpu.VMEM((2, BLOCK, KEY_VALUE_HEADS * HEAD_SIZE), BF16),
            pltpu.VMEM((N, HEADS, 2 * BLOCK), F32),
            pltpu.VMEM((N, HEADS, 2 * BLOCK), F32),
            pltpu.VMEM((2 * HEADS, ROWS), F32),
            full(HEADS, 2),
            full(2),
            full(2),
            pltpu.VMEM((HEAD_SIZE, ROWS), BF16),
            pltpu.VMEM((HEAD_SIZE, HALF), BF16),
            half(2),
            pltpu.VMEM((HEAD_SIZE, HALF), BF16),
            pltpu.VMEM((2, ROWS, HEAD_SIZE), F32),
            pltpu.VMEM((2, HALF, HEAD_SIZE), F32),
            pltpu.VMEM((2, HALF, HEAD_SIZE), F32),
            pltpu.VMEM((HEADS, HEAD_SIZE, ROWS), F32),
            full(HEADS),
            half(2),
            half(2),
            half(),
            half(),
            pltpu.VMEM((N // PIECES // 2, PIECES, BLOCK, HEAD_SIZE), BF16),
            pltpu.VMEM((N // PIECES // 2, PIECES, BLOCK, HEAD_SIZE), BF16),
            full(),
            full(),
            parts,
            dma((6,)),
            dma, dma, dma, dma, dma, dma, dma, dma, dma, dma,
            dma((HEADS,)), dma((HEADS,)),
            dma((2,)), dma((2,)), dma((PIECES + 1,)), dma((PIECES + 1,)), dma, dma, dma, dma, dma, dma,
        ],
        compiler_params=pltpu.CompilerParams(
            collective_id=1, has_side_effects=True, vmem_limit_bytes=48 << 20
        ),
        name="attention_backward",
    )(*inputs)
    return pl.pallas_call(
        flush,
        out_shape=(
            pltpu.HBM((BLOCK, HQ * HEAD_SIZE), BF16),
            pltpu.HBM((BLOCK, KEY_VALUE_HEADS * HEAD_SIZE), BF16),
            pltpu.HBM((BLOCK, KEY_VALUE_HEADS * HEAD_SIZE), BF16),
        ),
        in_specs=[vmem] * 2,
        out_specs=(hbm,) * 3,
        scratch_shapes=[dma((3,))],
        name="store_results",
    )(*(pltpu.with_memory_space_constraint(x, pltpu.VMEM) for x in (qg, kvg)))


def solution(mesh):
    tokens = P(("head", "ctx"), None)
    return jax.shard_map(
        shards,
        mesh=mesh,
        in_specs=(tokens,) * 6 + (P(),),
        out_specs=(tokens,) * 3,
        check_vma=False,
    )
```

```python
import jax
import jax.numpy as jnp
from jax import lax
from jax.experimental import pallas as pl
from jax.experimental.pallas import tpu as pltpu
from jax.sharding import PartitionSpec as P

HQ = 64
KEY_VALUE_HEADS = 8
HEAD_SIZE = 128
BLOCK = 64
N = 16
HEADS = HQ // N
ROWS = N * BLOCK
HALF = ROWS // 2
QUARTER = ROWS // 4
PIECES = 4
ORDER = [(x, y, c) for x, y in ((1, 2), (0, 2), (1, 1), (1, 3), (0, 1), (0, 3), (1, 0)) for c in (0, 1)] + [(0, 0, 1)]
FACTOR = HEAD_SIZE**-0.5
LOG2E = 1.4426950408889634
MESH = pl.DeviceIdType.MESH
F32 = jnp.float32
BF16 = jnp.bfloat16


def every(f):
    for s in range(1, N):
        f(s)


def dot(a, b):
    return jnp.dot(a, b, preferred_element_type=F32)


def dot_t(a, b):
    return lax.dot_general(a, b, (((1,), (1,)), ((), ())), preferred_element_type=F32)


def transposed(x):
    return x.T


def scores(k, v, q, do):
    return dot_t(k, q), dot_t(v, do)


def terms(front, kt, q, do, norm, delta, diagonal):
    s, dp = front
    p = jnp.exp2(s * (FACTOR * LOG2E) - norm)
    if diagonal:
        key = lax.broadcasted_iota(jnp.int32, s.shape, 0)
        query = lax.broadcasted_iota(jnp.int32, s.shape, 1)
        p = jnp.where(query >= key, p, 0.0)
    ds = (p * (dp - delta)).astype(BF16)
    p = p.astype(BF16)
    dv = dot(p, do)
    dk = dot(ds, q)
    return dot(kt, ds), dk, dv


def in_turn(tiles):
    ahead = scores(*tiles[0][0])
    for n, (_, rest, keep) in enumerate(tiles):
        front = ahead
        if n + 1 < len(tiles):
            ahead = scores(*tiles[n + 1][0])
        keep(*terms(front, *rest))


def kernel(
    q, do, at, k, v, log_norm, block_pos,
    qg, kvg,
    ln, bp, dov, atv, kvs, st_s, st_r, srow, qd, own, prev, own_t, prev_t, sel, sel_t,
    acc_own, acc_prev, acc_sel, dq_t, dq_s, x_s, x_r, back_s, back_r, ctx_s, ctx_r, y_s, y_r, fin,
    s_load, s_kv, r_kv, s_fw, r_fw, s_ctx, r_ctx, s_fwp, r_fwp, s_st, r_st, s_qd, r_qd,
    s_x, r_x, s_back, r_back, s_y, r_y, s_dq, r_dq, s_fin, r_fin,
):
    h = lax.axis_index("head")
    c = lax.axis_index("ctx")
    shift = lax.div(c, N // 2) * (N // 2)
    mine = lax.rem(h + shift, N)
    g = lax.div(mine, 2)
    m = lax.rem(h, 2)
    mate = h + 1 - 2 * m
    after = lax.rem(c + 1, N)
    before = lax.rem(c + N - 1, N)
    h_after = lax.rem(h + lax.div(lax.rem(c, N // 2) + 1, N // 2) * (N // 2), N)
    h_before = lax.rem(h + lax.div(lax.rem(before, N // 2) + 1, N // 2) * (N // 2), N)

    def remote(src, dst, ssem, rsem, **where):
        return pltpu.make_async_remote_copy(
            src_ref=src, dst_ref=dst, send_sem=ssem, recv_sem=rsem, device_id=where, device_id_type=MESH
        )

    def wait(ref, sem):
        pltpu.make_async_copy(ref, ref, sem).wait()

    def partner(s):
        x, y, core = ORDER[s - 1]
        chip_y = lax.rem(lax.rem(lax.div(h, 2), 4) + y, 4)
        chip_x = lax.rem(lax.div(h, 8) + x, 2)
        return chip_x * 8 + chip_y * 2 + lax.rem(h + core, 2)

    def cols(j):
        return pl.ds(pl.multiple_of(j * HEAD_SIZE, HEAD_SIZE), HEAD_SIZE)

    def rows(j):
        return pl.ds(pl.multiple_of(j * BLOCK, BLOCK), BLOCK)

    loads = [
        pltpu.make_async_copy(k, kvs.at[0], s_load.at[0]),
        pltpu.make_async_copy(v, kvs.at[1], s_load.at[1]),
        pltpu.make_async_copy(do, dov, s_load.at[2]),
        pltpu.make_async_copy(at, atv, s_load.at[3]),
        pltpu.make_async_copy(log_norm, ln, s_load.at[4]),
        pltpu.make_async_copy(block_pos, bp, s_load.at[5]),
    ]
    for copy in loads:
        copy.start()

    barrier = pltpu.get_barrier_semaphore()

    @pl.loop(1, N)
    def _(s):
        pl.semaphore_signal(barrier, inc=1, device_id={"head": lax.rem(h + s, N)}, device_id_type=MESH)

    pl.semaphore_signal(barrier, inc=1, device_id={"head": h_before, "ctx": before}, device_id_type=MESH)
    loads[0].wait()
    loads[1].wait()
    pl.semaphore_wait(barrier, N)

    @every
    def _(s):
        d = partner(s)
        e = lax.rem(d, 2)
        remote(kvs.at[e, :, cols(lax.div(lax.rem(d + shift, N), 2))], own.at[e, rows(h)], s_kv, r_kv, head=d).start()

    pltpu.make_async_copy(kvs.at[m, :, cols(g)], own.at[m, rows(h)], r_kv).start()

    def send_head(i):
        @every
        def _(s):
            d = partner(s)
            for which, ref in ((0, q), (1, do)):
                remote(
                    ref.at[:, cols(lax.rem(d + shift, N) * HEADS + i)], qd.at[i, which, rows(h)], s_qd.at[i], r_qd.at[i], head=d
                ).start()

        for which, ref in ((0, q), (1, do)):
            pltpu.make_async_copy(ref.at[:, cols(mine * HEADS + i)], qd.at[i, which, rows(h)], r_qd.at[i]).start()

    send_head(0)

    for copy in loads[2:]:
        copy.wait()
    lane = lax.broadcasted_iota(jnp.int32, (BLOCK, 2 * BLOCK), 1)

    def inner(j, total):
        part = jnp.sum(dov[:, cols(j)].astype(F32) * atv[:, cols(j)].astype(F32), axis=1, keepdims=True)
        return jnp.where(lane == j, part, total)

    deltas = lax.fori_loop(0, HQ, inner, jnp.zeros((BLOCK, 2 * BLOCK), F32), unroll=8)
    stats = jnp.where(lane < BLOCK, deltas, jnp.concatenate([ln[...], ln[...]], axis=1) * LOG2E).T
    stats = jnp.concatenate([stats[:HQ], stats[HQ:]], axis=1)
    for d in range(N):
        st_s[d] = stats[d * HEADS : (d + 1) * HEADS]

    @every
    def _(s):
        d = partner(s)
        remote(st_s.at[lax.rem(d + shift, N)], st_r.at[h], s_st, r_st, head=d).start()

    pltpu.make_async_copy(st_s.at[mine], st_r.at[h], r_st).start()

    wait(own.at[0], r_kv)
    forward = remote(own.at[m], own.at[m], s_fw, r_fw, head=mate)
    forward.start()
    onward = remote(own.at[m], prev.at[m], s_ctx, r_ctx, head=h_after, ctx=after)
    onward.start()

    @pl.loop(1, HEADS)
    def _(i):
        send_head(i)

    forward.wait_recv()
    own_t[...] = transposed(own[0])

    wait(st_r, r_st)
    for pair in range(N // 2):
        a, b = st_r[2 * pair], st_r[2 * pair + 1]
        at_pair = slice(pair * 2 * BLOCK, (pair + 1) * 2 * BLOCK)
        srow[:HEADS, at_pair] = jnp.concatenate([a[:, BLOCK:], b[:, BLOCK:]], axis=1)
        srow[HEADS:, at_pair] = jnp.concatenate([a[:, :BLOCK], b[:, :BLOCK]], axis=1)

    acc_own[...] = jnp.zeros_like(acc_own)
    acc_prev[...] = jnp.zeros_like(acc_prev)
    acc_sel[...] = jnp.zeros_like(acc_sel)
    dq_t[...] = jnp.zeros_like(dq_t)
    early = bp[c] > bp[before]

    def share_prev():
        return remote(prev.at[m], prev.at[m], s_fwp, r_fwp, head=mate)

    def take_prev():
        share_prev().wait_recv()
        for which in range(2):
            sel[which] = jnp.where(early, prev[which, :HALF], prev[which, HALF:])
        prev_t[...] = transposed(prev[0, :HALF])
        sel_t[...] = transposed(sel[0])

    def add(ref, lo, size, dk, dv):
        ref[0, lo : lo + size] += dk
        ref[1, lo : lo + size] += dv

    def pieces(x):
        return x.reshape(-1, PIECES, BLOCK, HEAD_SIZE)

    def row(i, lo, size):
        return srow[pl.ds(i, 1), lo : lo + size], srow[pl.ds(HEADS + i, 1), lo : lo + size]

    def swap(n):
        return remote(x_s.at[n], x_r.at[n], s_x.at[n], r_x.at[n], head=mate)

    def both_cores(ref, n):
        wait(x_r.at[n], r_x.at[n])
        scale = jnp.where(m == 0, FACTOR, 1.0)
        return ((ref[m] + x_r[n].astype(F32)) * scale).astype(BF16)

    def other_tiles(i):
        n0, d0 = row(i, 0, HALF)
        n1, d1 = row(i, HALF, HALF)
        q_sel = jnp.where(early, qd[i, 0, :HALF], qd[i, 0, HALF:])
        do_sel = jnp.where(early, qd[i, 1, :HALF], qd[i, 1, HALF:])
        n_sel, d_sel = jnp.where(early, n0, n1), jnp.where(early, d0, d1)
        q1, do1 = qd[i, 0, HALF:], qd[i, 1, HALF:]

        def keep_sel(dq, dk, dv):
            add(acc_sel, 0, HALF, dk, dv)
            zero = jnp.zeros_like(dq)
            dq_t[i, :, :HALF] += jnp.where(early, dq, zero)
            dq_t[i, :, HALF:] += jnp.where(early, zero, dq)

        def keep_prev(dq, dk, dv):
            add(acc_prev, 0, HALF, dk, dv)
            dq_t[i, :, HALF:] += dq

        return (
            ((prev[0, :HALF], prev[1, :HALF], q1, do1), (prev_t[...], q1, do1, n1, d1, False), keep_prev),
            ((sel[0], sel[1], q_sel, do_sel), (sel_t[...], q_sel, do_sel, n_sel, d_sel, False), keep_sel),
        )

    def own_tile(i, k0, k1, q0, q1, diagonal):
        q, do = qd[i, 0, q0:q1], qd[i, 1, q0:q1]
        norm, delta = row(i, q0, q1 - q0)

        def keep(dq, dk, dv):
            add(acc_own, k0, k1 - k0, dk, dv)
            dq_t[i, :, q0:q1] += dq

        return (own[0, k0:k1], own[1, k0:k1], q, do), (own_t[:, k0:k1], q, do, norm, delta, diagonal), keep

    def own_group(i):
        in_turn([
            own_tile(i, 0, HALF, HALF, ROWS, False),
            own_tile(i, 0, QUARTER, 0, HALF, True),
            own_tile(i, QUARTER, HALF, QUARTER, HALF, True),
            own_tile(i, HALF, HALF + QUARTER, HALF, ROWS, True),
            own_tile(i, HALF + QUARTER, ROWS, HALF + QUARTER, ROWS, True),
        ])

    def round_dq(i):
        dq_s[i] = (dq_t[i] * FACTOR).astype(BF16).T

    def send_dq(i):
        @every
        def _(s):
            d = partner(s)
            remote(dq_s.at[i, rows(d)], qg.at[:, cols(mine * HEADS + i)], s_dq, r_dq, head=d).start()

        pltpu.make_async_copy(dq_s.at[i, rows(h)], qg.at[:, cols(mine * HEADS + i)], r_dq).start()

    @pl.loop(0, 2 * HEADS)
    def _(t):
        i = jnp.where(t < 4, lax.rem(t, 2), lax.div(t, 2))
        first = (t < 2) | (t == 4) | (t == 6)
        is_own = (t < 2) | (t == 4) | (t == 7)

        @pl.when(first)
        def _():
            wait(qd.at[i], r_qd.at[i])

        @pl.when(t == 1)
        def _():
            onward.wait_recv()
            share_prev().start()

        @pl.when(t == 2)
        def _():
            take_prev()

        @pl.when(jnp.logical_not(is_own | (t == 6)))
        def _():
            in_turn(other_tiles(i))

        @pl.when(t == 6)
        def _():
            for n, (spec, ref) in enumerate(zip(other_tiles(i), (acc_prev, acc_sel))):
                in_turn([spec])
                x_s[n] = ref[1 - m].astype(BF16)
                swap(n).start()
            back_s[...] = both_cores(acc_prev, 0)
            remote(back_s, back_r, s_back.at[PIECES], r_back.at[PIECES], head=h_before, ctx=before).start()
            round_dq(i - 1)
            chosen = pieces(both_cores(acc_sel, 1))
            for e in range(PIECES):
                ctx_s[:, e] = chosen[:, e]
                remote(
                    ctx_s.at[:, e], ctx_r.at[:, e], s_back.at[e], r_back.at[e], head=h_before, ctx=before
                ).start()
            send_dq(i - 1)

        @pl.when(is_own)
        def _():
            own_group(i)

        @pl.when(jnp.logical_not(first | (t == 5)))
        def _():
            round_dq(i)
            send_dq(i)

    y_s[...] = acc_own[1 - m].astype(BF16)
    remote(y_s, y_r, s_y, r_y, head=mate).start()
    scale = jnp.where(m == 0, FACTOR, 1.0)
    wait(y_r, r_y)
    total = pieces((acc_own[m] + y_r[...].astype(F32)) * scale)
    next_early = bp[after] > bp[c]
    wait(back_r, r_back.at[PIECES])
    low = total[: N // PIECES // 2] + pieces(back_r[...]).astype(F32)
    high = total[N // PIECES // 2 :]
    for e in range(PIECES):
        wait(ctx_r.at[:, e], r_back.at[e])
        chosen = ctx_r[:, e].astype(F32)
        zero = jnp.zeros_like(chosen)
        fin[: N // PIECES // 2, e] = (low[:, e] + jnp.where(next_early, chosen, zero)).astype(BF16)
        fin[N // PIECES // 2 :, e] = (high[:, e] + jnp.where(next_early, zero, chosen)).astype(BF16)

        @pl.loop(0, N // PIECES)
        def _(s):
            t = lax.rem(lax.div(h, PIECES) + (N // PIECES - 1) - s, N // PIECES)
            d = t * PIECES + e

            @pl.when(d != h)
            def _():
                remote(fin.at[t, e], kvg.at[m, :, cols(g)], s_fin, r_fin, head=d).start()

            @pl.when(d == h)
            def _():
                pltpu.make_async_copy(fin.at[t, e], kvg.at[m, :, cols(g)], r_fin).start()

    most = (N - 1) * BLOCK
    wait(own.at[0, :most], s_kv)
    forward.wait_send()
    onward.wait_send()
    wait(prev.at[0], s_fwp)
    wait(st_r.at[: N - 1], s_st)
    for i in range(HEADS):
        wait(qd.at[i, :, :most], s_qd.at[i])
    for n in range(2):
        wait(x_s.at[n], s_x.at[n])
    wait(back_s, s_back.at[PIECES])
    for e in range(PIECES):
        wait(ctx_s.at[:, e], s_back.at[e])
    wait(y_s, s_y)
    wait(dq_s.at[:, :most], s_dq)
    wait(own.at[0, :most], s_fin)
    wait(qg, r_dq)
    wait(kvg, r_fin)


def flush(qg, kvg, query_grad, key_gradient, value_gradient, sem):
    copies = [
        pltpu.make_async_copy(qg, query_grad, sem.at[0]),
        pltpu.make_async_copy(kvg.at[0], key_gradient, sem.at[1]),
        pltpu.make_async_copy(kvg.at[1], value_gradient, sem.at[2]),
    ]
    for copy in copies:
        copy.start()
    for copy in copies:
        copy.wait()


def shards(query_states, saved_key_rows, saved_value_rows, attn_output, out_grad, log_norm, block_pos):
    hbm = pl.BlockSpec(memory_space=pltpu.HBM)
    vmem = pl.BlockSpec(memory_space=pltpu.VMEM)
    inputs = (query_states, out_grad, attn_output, saved_key_rows, saved_value_rows, log_norm, block_pos)
    inputs = tuple(pltpu.with_memory_space_constraint(x, pltpu.HBM) for x in inputs)
    dma = pltpu.SemaphoreType.DMA
    half = lambda *lead: pltpu.VMEM((*lead, HALF, HEAD_SIZE), BF16)
    parts = pltpu.VMEM((N // PIECES, PIECES, BLOCK, HEAD_SIZE), BF16)
    full = lambda *lead: pltpu.VMEM((*lead, ROWS, HEAD_SIZE), BF16)
    qg, kvg = pl.pallas_call(
        kernel,
        out_shape=(
            pltpu.VMEM((BLOCK, HQ * HEAD_SIZE), BF16),
            pltpu.VMEM((2, BLOCK, KEY_VALUE_HEADS * HEAD_SIZE), BF16),
        ),
        in_specs=[hbm] * 7,
        out_specs=(vmem, vmem),
        scratch_shapes=[
            pltpu.VMEM((BLOCK, HQ), F32),
            pltpu.SMEM((N * N,), jnp.int32),
            pltpu.VMEM((BLOCK, HQ * HEAD_SIZE), BF16),
            pltpu.VMEM((BLOCK, HQ * HEAD_SIZE), BF16),
            pltpu.VMEM((2, BLOCK, KEY_VALUE_HEADS * HEAD_SIZE), BF16),
            pltpu.VMEM((N, HEADS, 2 * BLOCK), F32),
            pltpu.VMEM((N, HEADS, 2 * BLOCK), F32),
            pltpu.VMEM((2 * HEADS, ROWS), F32),
            full(HEADS, 2),
            full(2),
            full(2),
            pltpu.VMEM((HEAD_SIZE, ROWS), BF16),
            pltpu.VMEM((HEAD_SIZE, HALF), BF16),
            half(2),
            pltpu.VMEM((HEAD_SIZE, HALF), BF16),
            pltpu.VMEM((2, ROWS, HEAD_SIZE), F32),
            pltpu.VMEM((2, HALF, HEAD_SIZE), F32),
            pltpu.VMEM((2, HALF, HEAD_SIZE), F32),
            pltpu.VMEM((HEADS, HEAD_SIZE, ROWS), F32),
            full(HEADS),
            half(2),
            half(2),
            half(),
            half(),
            pltpu.VMEM((N // PIECES // 2, PIECES, BLOCK, HEAD_SIZE), BF16),
            pltpu.VMEM((N // PIECES // 2, PIECES, BLOCK, HEAD_SIZE), BF16),
            full(),
            full(),
            parts,
            dma((6,)),
            dma, dma, dma, dma, dma, dma, dma, dma, dma, dma,
            dma((HEADS,)), dma((HEADS,)),
            dma((2,)), dma((2,)), dma((PIECES + 1,)), dma((PIECES + 1,)), dma, dma, dma, dma, dma, dma,
        ],
        compiler_params=pltpu.CompilerParams(
            collective_id=1, has_side_effects=True, vmem_limit_bytes=48 << 20
        ),
        name="attention_backward",
    )(*inputs)
    return pl.pallas_call(
        flush,
        out_shape=(
            pltpu.HBM((BLOCK, HQ * HEAD_SIZE), BF16),
            pltpu.HBM((BLOCK, KEY_VALUE_HEADS * HEAD_SIZE), BF16),
            pltpu.HBM((BLOCK, KEY_VALUE_HEADS * HEAD_SIZE), BF16),
        ),
        in_specs=[vmem] * 2,
        out_specs=(hbm,) * 3,
        scratch_shapes=[dma((3,))],
        name="store_results",
    )(*(pltpu.with_memory_space_constraint(x, pltpu.VMEM) for x in (qg, kvg)))


def solution(mesh):
    tokens = P(("head", "ctx"), None)
    return jax.shard_map(
        shards,
        mesh=mesh,
        in_specs=(tokens,) * 6 + (P(),),
        out_specs=(tokens,) * 3,
        check_vma=False,
    )
```

```python
import jax
import jax.numpy as jnp
from jax import lax
from jax.experimental import pallas as pl
from jax.experimental.pallas import tpu as pltpu
from jax.sharding import PartitionSpec as P

HQ = 64
KEY_VALUE_HEADS = 8
HEAD_SIZE = 128
BLOCK = 64
N = 16
HEADS = HQ // N
ROWS = N * BLOCK
HALF = ROWS // 2
QUARTER = ROWS // 4
PIECES = 8
ORDER = [(x, y, c) for x, y in ((1, 2), (0, 2), (1, 1), (1, 3), (0, 1), (0, 3), (1, 0)) for c in (0, 1)] + [(0, 0, 1)]
FACTOR = HEAD_SIZE**-0.5
LOG2E = 1.4426950408889634
MESH = pl.DeviceIdType.MESH
F32 = jnp.float32
BF16 = jnp.bfloat16


def every(f):
    for s in range(1, N):
        f(s)


def dot(a, b):
    return jnp.dot(a, b, preferred_element_type=F32)


def dot_t(a, b):
    return lax.dot_general(a, b, (((1,), (1,)), ((), ())), preferred_element_type=F32)


def transposed(x):
    return x.T


def scores(k, v, q, do):
    return dot_t(k, q), dot_t(v, do)


def terms(front, kt, q, do, norm, delta, diagonal):
    s, dp = front
    p = jnp.exp2(s * (FACTOR * LOG2E) - norm)
    if diagonal:
        key = lax.broadcasted_iota(jnp.int32, s.shape, 0)
        query = lax.broadcasted_iota(jnp.int32, s.shape, 1)
        p = jnp.where(query >= key, p, 0.0)
    ds = (p * (dp - delta)).astype(BF16)
    p = p.astype(BF16)
    dv = dot(p, do)
    dk = dot(ds, q)
    return dot(kt, ds), dk, dv


def in_turn(tiles):
    ahead = scores(*tiles[0][0])
    for n, (_, rest, keep) in enumerate(tiles):
        front = ahead
        if n + 1 < len(tiles):
            ahead = scores(*tiles[n + 1][0])
        keep(*terms(front, *rest))


def kernel(
    q, do, at, k, v, log_norm, block_pos,
    qg, kvg,
    ln, bp, dov, atv, kvs, st_s, st_r, srow, qd, own, prev, own_t, prev_t, sel, sel_t,
    acc_own, acc_prev, acc_sel, dq_t, dq_s, x_s, x_r, back_s, back_r, ctx_s, ctx_r, y_s, y_r, fin,
    s_load, s_kv, r_kv, s_fw, r_fw, s_ctx, r_ctx, s_fwp, r_fwp, s_st, r_st, s_qd, r_qd,
    s_x, r_x, s_back, r_back, s_y, r_y, s_dq, r_dq, s_fin, r_fin,
):
    h = lax.axis_index("head")
    c = lax.axis_index("ctx")
    shift = lax.div(c, N // 2) * (N // 2)
    mine = lax.rem(h + shift, N)
    g = lax.div(mine, 2)
    m = lax.rem(h, 2)
    mate = h + 1 - 2 * m
    after = lax.rem(c + 1, N)
    before = lax.rem(c + N - 1, N)
    h_after = lax.rem(h + lax.div(lax.rem(c, N // 2) + 1, N // 2) * (N // 2), N)
    h_before = lax.rem(h + lax.div(lax.rem(before, N // 2) + 1, N // 2) * (N // 2), N)

    def remote(src, dst, ssem, rsem, **where):
        return pltpu.make_async_remote_copy(
            src_ref=src, dst_ref=dst, send_sem=ssem, recv_sem=rsem, device_id=where, device_id_type=MESH
        )

    def wait(ref, sem):
        pltpu.make_async_copy(ref, ref, sem).wait()

    def partner(s):
        x, y, core = ORDER[s - 1]
        chip_y = lax.rem(lax.rem(lax.div(h, 2), 4) + y, 4)
        chip_x = lax.rem(lax.div(h, 8) + x, 2)
        return chip_x * 8 + chip_y * 2 + lax.rem(h + core, 2)

    def cols(j):
        return pl.ds(pl.multiple_of(j * HEAD_SIZE, HEAD_SIZE), HEAD_SIZE)

    def rows(j):
        return pl.ds(pl.multiple_of(j * BLOCK, BLOCK), BLOCK)

    loads = [
        pltpu.make_async_copy(k, kvs.at[0], s_load.at[0]),
        pltpu.make_async_copy(v, kvs.at[1], s_load.at[1]),
        pltpu.make_async_copy(do, dov, s_load.at[2]),
        pltpu.make_async_copy(at, atv, s_load.at[3]),
        pltpu.make_async_copy(log_norm, ln, s_load.at[4]),
        pltpu.make_async_copy(block_pos, bp, s_load.at[5]),
    ]
    for copy in loads:
        copy.start()

    barrier = pltpu.get_barrier_semaphore()

    @pl.loop(1, N)
    def _(s):
        pl.semaphore_signal(barrier, inc=1, device_id={"head": lax.rem(h + s, N)}, device_id_type=MESH)

    pl.semaphore_signal(barrier, inc=1, device_id={"head": h_before, "ctx": before}, device_id_type=MESH)
    loads[0].wait()
    loads[1].wait()
    pl.semaphore_wait(barrier, N)

    @every
    def _(s):
        d = partner(s)
        e = lax.rem(d, 2)
        remote(kvs.at[e, :, cols(lax.div(lax.rem(d + shift, N), 2))], own.at[e, rows(h)], s_kv, r_kv, head=d).start()

    pltpu.make_async_copy(kvs.at[m, :, cols(g)], own.at[m, rows(h)], r_kv).start()

    def send_head(i):
        @every
        def _(s):
            d = partner(s)
            for which, ref in ((0, q), (1, do)):
                remote(
                    ref.at[:, cols(lax.rem(d + shift, N) * HEADS + i)], qd.at[i, which, rows(h)], s_qd.at[i], r_qd.at[i], head=d
                ).start()

        for which, ref in ((0, q), (1, do)):
            pltpu.make_async_copy(ref.at[:, cols(mine * HEADS + i)], qd.at[i, which, rows(h)], r_qd.at[i]).start()

    send_head(0)

    for copy in loads[2:]:
        copy.wait()
    lane = lax.broadcasted_iota(jnp.int32, (BLOCK, 2 * BLOCK), 1)

    def inner(j, total):
        part = jnp.sum(dov[:, cols(j)].astype(F32) * atv[:, cols(j)].astype(F32), axis=1, keepdims=True)
        return jnp.where(lane == j, part, total)

    deltas = lax.fori_loop(0, HQ, inner, jnp.zeros((BLOCK, 2 * BLOCK), F32), unroll=8)
    stats = jnp.where(lane < BLOCK, deltas, jnp.concatenate([ln[...], ln[...]], axis=1) * LOG2E).T
    stats = jnp.concatenate([stats[:HQ], stats[HQ:]], axis=1)
    for d in range(N):
        st_s[d] = stats[d * HEADS : (d + 1) * HEADS]

    @every
    def _(s):
        d = partner(s)
        remote(st_s.at[lax.rem(d + shift, N)], st_r.at[h], s_st, r_st, head=d).start()

    pltpu.make_async_copy(st_s.at[mine], st_r.at[h], r_st).start()

    wait(own.at[0], r_kv)
    forward = remote(own.at[m], own.at[m], s_fw, r_fw, head=mate)
    forward.start()
    onward = remote(own.at[m], prev.at[m], s_ctx, r_ctx, head=h_after, ctx=after)
    onward.start()

    @pl.loop(1, HEADS)
    def _(i):
        send_head(i)

    forward.wait_recv()
    own_t[...] = transposed(own[0])

    wait(st_r, r_st)
    for pair in range(N // 2):
        a, b = st_r[2 * pair], st_r[2 * pair + 1]
        at_pair = slice(pair * 2 * BLOCK, (pair + 1) * 2 * BLOCK)
        srow[:HEADS, at_pair] = jnp.concatenate([a[:, BLOCK:], b[:, BLOCK:]], axis=1)
        srow[HEADS:, at_pair] = jnp.concatenate([a[:, :BLOCK], b[:, :BLOCK]], axis=1)

    acc_own[...] = jnp.zeros_like(acc_own)
    acc_prev[...] = jnp.zeros_like(acc_prev)
    acc_sel[...] = jnp.zeros_like(acc_sel)
    dq_t[...] = jnp.zeros_like(dq_t)
    early = bp[c] > bp[before]

    def share_prev():
        return remote(prev.at[m], prev.at[m], s_fwp, r_fwp, head=mate)

    def take_prev():
        share_prev().wait_recv()
        for which in range(2):
            sel[which] = jnp.where(early, prev[which, :HALF], prev[which, HALF:])
        prev_t[...] = transposed(prev[0, :HALF])
        sel_t[...] = transposed(sel[0])

    def add(ref, lo, size, dk, dv):
        ref[0, lo : lo + size] += dk
        ref[1, lo : lo + size] += dv

    def pieces(x):
        return x.reshape(-1, PIECES, BLOCK, HEAD_SIZE)

    def row(i, lo, size):
        return srow[pl.ds(i, 1), lo : lo + size], srow[pl.ds(HEADS + i, 1), lo : lo + size]

    def swap(n):
        return remote(x_s.at[n], x_r.at[n], s_x.at[n], r_x.at[n], head=mate)

    def both_cores(ref, n):
        wait(x_r.at[n], r_x.at[n])
        scale = jnp.where(m == 0, FACTOR, 1.0)
        return ((ref[m] + x_r[n].astype(F32)) * scale).astype(BF16)

    def other_tiles(i):
        n0, d0 = row(i, 0, HALF)
        n1, d1 = row(i, HALF, HALF)
        q_sel = jnp.where(early, qd[i, 0, :HALF], qd[i, 0, HALF:])
        do_sel = jnp.where(early, qd[i, 1, :HALF], qd[i, 1, HALF:])
        n_sel, d_sel = jnp.where(early, n0, n1), jnp.where(early, d0, d1)
        q1, do1 = qd[i, 0, HALF:], qd[i, 1, HALF:]

        def keep_sel(dq, dk, dv):
            add(acc_sel, 0, HALF, dk, dv)
            zero = jnp.zeros_like(dq)
            dq_t[i, :, :HALF] += jnp.where(early, dq, zero)
            dq_t[i, :, HALF:] += jnp.where(early, zero, dq)

        def keep_prev(dq, dk, dv):
            add(acc_prev, 0, HALF, dk, dv)
            dq_t[i, :, HALF:] += dq

        return (
            ((prev[0, :HALF], prev[1, :HALF], q1, do1), (prev_t[...], q1, do1, n1, d1, False), keep_prev),
            ((sel[0], sel[1], q_sel, do_sel), (sel_t[...], q_sel, do_sel, n_sel, d_sel, False), keep_sel),
        )

    def own_tile(i, k0, k1, q0, q1, diagonal):
        q, do = qd[i, 0, q0:q1], qd[i, 1, q0:q1]
        norm, delta = row(i, q0, q1 - q0)

        def keep(dq, dk, dv):
            add(acc_own, k0, k1 - k0, dk, dv)
            dq_t[i, :, q0:q1] += dq

        return (own[0, k0:k1], own[1, k0:k1], q, do), (own_t[:, k0:k1], q, do, norm, delta, diagonal), keep

    def own_group(i):
        in_turn([
            own_tile(i, 0, HALF, HALF, ROWS, False),
            own_tile(i, 0, QUARTER, 0, HALF, True),
            own_tile(i, QUARTER, HALF, QUARTER, HALF, True),
            own_tile(i, HALF, HALF + QUARTER, HALF, ROWS, True),
            own_tile(i, HALF + QUARTER, ROWS, HALF + QUARTER, ROWS, True),
        ])

    def round_dq(i):
        dq_s[i] = (dq_t[i] * FACTOR).astype(BF16).T

    def send_dq(i):
        @every
        def _(s):
            d = partner(s)
            remote(dq_s.at[i, rows(d)], qg.at[:, cols(mine * HEADS + i)], s_dq, r_dq, head=d).start()

        pltpu.make_async_copy(dq_s.at[i, rows(h)], qg.at[:, cols(mine * HEADS + i)], r_dq).start()

    @pl.loop(0, 2 * HEADS)
    def _(t):
        i = jnp.where(t < 4, lax.rem(t, 2), lax.div(t, 2))
        first = (t < 2) | (t == 4) | (t == 6)
        is_own = (t < 2) | (t == 4) | (t == 7)

        @pl.when(first)
        def _():
            wait(qd.at[i], r_qd.at[i])

        @pl.when(t == 1)
        def _():
            onward.wait_recv()
            share_prev().start()

        @pl.when(t == 2)
        def _():
            take_prev()

        @pl.when(jnp.logical_not(is_own | (t == 6)))
        def _():
            in_turn(other_tiles(i))

        @pl.when(t == 6)
        def _():
            for n, (spec, ref) in enumerate(zip(other_tiles(i), (acc_prev, acc_sel))):
                in_turn([spec])
                x_s[n] = ref[1 - m].astype(BF16)
                swap(n).start()
            back_s[...] = both_cores(acc_prev, 0)
            remote(back_s, back_r, s_back.at[PIECES], r_back.at[PIECES], head=h_before, ctx=before).start()
            round_dq(i - 1)
            chosen = pieces(both_cores(acc_sel, 1))
            for e in range(PIECES):
                ctx_s[:, e] = chosen[:, e]
                remote(
                    ctx_s.at[:, e], ctx_r.at[:, e], s_back.at[e], r_back.at[e], head=h_before, ctx=before
                ).start()
            send_dq(i - 1)

        @pl.when(is_own)
        def _():
            own_group(i)

        @pl.when(jnp.logical_not(first | (t == 5)))
        def _():
            round_dq(i)
            send_dq(i)

    y_s[...] = acc_own[1 - m].astype(BF16)
    remote(y_s, y_r, s_y, r_y, head=mate).start()
    scale = jnp.where(m == 0, FACTOR, 1.0)
    wait(y_r, r_y)
    total = pieces((acc_own[m] + y_r[...].astype(F32)) * scale)
    next_early = bp[after] > bp[c]
    wait(back_r, r_back.at[PIECES])
    low = total[: N // PIECES // 2] + pieces(back_r[...]).astype(F32)
    high = total[N // PIECES // 2 :]
    for e in range(PIECES):
        wait(ctx_r.at[:, e], r_back.at[e])
        chosen = ctx_r[:, e].astype(F32)
        zero = jnp.zeros_like(chosen)
        fin[: N // PIECES // 2, e] = (low[:, e] + jnp.where(next_early, chosen, zero)).astype(BF16)
        fin[N // PIECES // 2 :, e] = (high[:, e] + jnp.where(next_early, zero, chosen)).astype(BF16)

        @pl.loop(0, N // PIECES)
        def _(s):
            t = lax.rem(lax.div(h, PIECES) + (N // PIECES - 1) - s, N // PIECES)
            d = t * PIECES + e

            @pl.when(d != h)
            def _():
                remote(fin.at[t, e], kvg.at[m, :, cols(g)], s_fin, r_fin, head=d).start()

            @pl.when(d == h)
            def _():
                pltpu.make_async_copy(fin.at[t, e], kvg.at[m, :, cols(g)], r_fin).start()

    most = (N - 1) * BLOCK
    wait(own.at[0, :most], s_kv)
    forward.wait_send()
    onward.wait_send()
    wait(prev.at[0], s_fwp)
    wait(st_r.at[: N - 1], s_st)
    for i in range(HEADS):
        wait(qd.at[i, :, :most], s_qd.at[i])
    for n in range(2):
        wait(x_s.at[n], s_x.at[n])
    wait(back_s, s_back.at[PIECES])
    for e in range(PIECES):
        wait(ctx_s.at[:, e], s_back.at[e])
    wait(y_s, s_y)
    wait(dq_s.at[:, :most], s_dq)
    wait(own.at[0, :most], s_fin)
    wait(qg, r_dq)
    wait(kvg, r_fin)


def flush(qg, kvg, query_grad, key_gradient, value_gradient, sem):
    copies = [
        pltpu.make_async_copy(qg, query_grad, sem.at[0]),
        pltpu.make_async_copy(kvg.at[0], key_gradient, sem.at[1]),
        pltpu.make_async_copy(kvg.at[1], value_gradient, sem.at[2]),
    ]
    for copy in copies:
        copy.start()
    for copy in copies:
        copy.wait()


def shards(query_states, saved_key_rows, saved_value_rows, attn_output, out_grad, log_norm, block_pos):
    hbm = pl.BlockSpec(memory_space=pltpu.HBM)
    vmem = pl.BlockSpec(memory_space=pltpu.VMEM)
    inputs = (query_states, out_grad, attn_output, saved_key_rows, saved_value_rows, log_norm, block_pos)
    inputs = tuple(pltpu.with_memory_space_constraint(x, pltpu.HBM) for x in inputs)
    dma = pltpu.SemaphoreType.DMA
    half = lambda *lead: pltpu.VMEM((*lead, HALF, HEAD_SIZE), BF16)
    parts = pltpu.VMEM((N // PIECES, PIECES, BLOCK, HEAD_SIZE), BF16)
    full = lambda *lead: pltpu.VMEM((*lead, ROWS, HEAD_SIZE), BF16)
    qg, kvg = pl.pallas_call(
        kernel,
        out_shape=(
            pltpu.VMEM((BLOCK, HQ * HEAD_SIZE), BF16),
            pltpu.VMEM((2, BLOCK, KEY_VALUE_HEADS * HEAD_SIZE), BF16),
        ),
        in_specs=[hbm] * 7,
        out_specs=(vmem, vmem),
        scratch_shapes=[
            pltpu.VMEM((BLOCK, HQ), F32),
            pltpu.SMEM((N * N,), jnp.int32),
            pltpu.VMEM((BLOCK, HQ * HEAD_SIZE), BF16),
            pltpu.VMEM((BLOCK, HQ * HEAD_SIZE), BF16),
            pltpu.VMEM((2, BLOCK, KEY_VALUE_HEADS * HEAD_SIZE), BF16),
            pltpu.VMEM((N, HEADS, 2 * BLOCK), F32),
            pltpu.VMEM((N, HEADS, 2 * BLOCK), F32),
            pltpu.VMEM((2 * HEADS, ROWS), F32),
            full(HEADS, 2),
            full(2),
            full(2),
            pltpu.VMEM((HEAD_SIZE, ROWS), BF16),
            pltpu.VMEM((HEAD_SIZE, HALF), BF16),
            half(2),
            pltpu.VMEM((HEAD_SIZE, HALF), BF16),
            pltpu.VMEM((2, ROWS, HEAD_SIZE), F32),
            pltpu.VMEM((2, HALF, HEAD_SIZE), F32),
            pltpu.VMEM((2, HALF, HEAD_SIZE), F32),
            pltpu.VMEM((HEADS, HEAD_SIZE, ROWS), F32),
            full(HEADS),
            half(2),
            half(2),
            half(),
            half(),
            pltpu.VMEM((N // PIECES // 2, PIECES, BLOCK, HEAD_SIZE), BF16),
            pltpu.VMEM((N // PIECES // 2, PIECES, BLOCK, HEAD_SIZE), BF16),
            full(),
            full(),
            parts,
            dma((6,)),
            dma, dma, dma, dma, dma, dma, dma, dma, dma, dma,
            dma((HEADS,)), dma((HEADS,)),
            dma((2,)), dma((2,)), dma((PIECES + 1,)), dma((PIECES + 1,)), dma, dma, dma, dma, dma, dma,
        ],
        compiler_params=pltpu.CompilerParams(
            collective_id=1, has_side_effects=True, vmem_limit_bytes=48 << 20
        ),
        name="attention_backward",
    )(*inputs)
    return pl.pallas_call(
        flush,
        out_shape=(
            pltpu.HBM((BLOCK, HQ * HEAD_SIZE), BF16),
            pltpu.HBM((BLOCK, KEY_VALUE_HEADS * HEAD_SIZE), BF16),
            pltpu.HBM((BLOCK, KEY_VALUE_HEADS * HEAD_SIZE), BF16),
        ),
        in_specs=[vmem] * 2,
        out_specs=(hbm,) * 3,
        scratch_shapes=[dma((3,))],
        name="store_results",
    )(*(pltpu.with_memory_space_constraint(x, pltpu.VMEM) for x in (qg, kvg)))


def solution(mesh):
    tokens = P(("head", "ctx"), None)
    return jax.shard_map(
        shards,
        mesh=mesh,
        in_specs=(tokens,) * 6 + (P(),),
        out_specs=(tokens,) * 3,
        check_vma=False,
    )
```
